512 devices in a mesh: ctx: 8 (over y), zero: 64 (over x, z, core).
Axes of the slice: x: 4, y: 8, z: 8, core: 2. Of those that a mesh axis runs over, the one named last changes fastest.
Arguments:
- logit_partial: float32 [8, 8, 64], P('ctx'), may hold values from 10 to 400
- head_order: int32 [8, 64], replicated, may hold values from 0 to 63, each once within a row
- query_weight: float32 [8, 1536, 12288], P('ctx', 'zero'), may hold values from -0.15625 to 0.15625
- query_moment: bfloat16 [8, 1536, 12288], P('ctx', 'zero'), may hold values from -6 to 6
- query_grad: bfloat16 [8, 1536, 12288], P('ctx', 'zero'), may hold values from -6 to 6
- key_weight: float32 [8, 512, 8192], P('ctx', 'zero'), may hold values from -0.25 to 0.25
- key_moment: bfloat16 [8, 512, 8192], P('ctx', 'zero'), may hold values from -6 to 6
- key_grad: bfloat16 [8, 512, 8192], P('ctx', 'zero'), may hold values from -6 to 6
Outputs:
- query_final: float32 [8, 1536, 12288], P('ctx', 'zero')
- query_velocity: bfloat16 [8, 1536, 12288], P('ctx', 'zero')
- key_final: float32 [8, 512, 8192], P('ctx', 'zero')
- key_velocity: bfloat16 [8, 512, 8192], P('ctx', 'zero')
The draws below stay inside these ranges and needn't reach their ends.
Inputs may be any that keep to these rules, and one draw needn't show every extreme that they name: `head_order`: each layer's row is a permutation of the 64 head numbers.
All inputs are finite; a program needn't handle non-finite values.
Results may differ from the reference program's by a relative error of at most 0.001.
Values may be sent and summed in bfloat16 or wider, within the bound.
A program may use at most 64 MiB of HBM per device.

```python
import math
import jax
import jax.numpy as jnp
from jax import lax

QR = 1536
KR = 512
HEADS = 64
NOPE = 128
ROPE = 64
ITERS = 5
LAYERS = 8
N_CTX = 8


def levels(stream_key, extent, split, low, largest):
    gain = 1.0
    for position, parts in split:
        steps = jax.random.uniform(jax.random.fold_in(jax.random.fold_in(stream_key, 6), position), (parts,), jnp.float32, low / len(split), largest / len(split))
        gain = gain * jnp.repeat(jnp.exp(steps), extent[position] // parts).reshape((-1,) + (1,) * (len(extent) - 1 - position))
    return gain


def centred(stream_key, extent, spread, reach, split=(), held_as=jnp.bfloat16):
    array = spread * jax.random.normal(stream_key, extent, jnp.float32)
    if split:
        array = array * levels(stream_key, extent, split, -0.22, 0.18)
    return jnp.clip(array, -reach, reach).astype(held_as)


def setup_inputs(seed: int = 0) -> dict:
    key_of = jax.random.split(jax.random.key(seed), 9)
    logit_partial = jnp.clip(jnp.exp(math.log(400.0) - 3.6888795 * jax.random.uniform(key_of[0], (N_CTX, LAYERS, HEADS), jnp.float32) ** levels(key_of[0], (N_CTX, LAYERS, HEADS), ((0, 8),), -0.2, 0.2)), 10.0, 400.0)
    head_order = jax.vmap(lambda own: jax.random.permutation(own, HEADS))(jax.random.split(key_of[1], LAYERS)).reshape((LAYERS, HEADS)).astype(jnp.int32)
    query_weight = centred(key_of[2], (LAYERS, QR, HEADS * (NOPE + ROPE)), QR ** -0.5, 0.15625, ((0, 8), (1, 64)), jnp.float32)
    query_moment = centred(key_of[3], (LAYERS, QR, HEADS * (NOPE + ROPE)), 1.0, 6.0, ((0, 8), (1, 64)))
    query_grad = centred(key_of[4], (LAYERS, QR, HEADS * (NOPE + ROPE)), 1.0, 6.0, ((0, 8), (1, 64)))
    key_weight = centred(key_of[5], (LAYERS, KR, HEADS * NOPE), KR ** -0.5, 0.25, ((0, 8), (1, 64)), jnp.float32)
    key_moment = centred(key_of[6], (LAYERS, KR, HEADS * NOPE), 1.0, 6.0, ((0, 8), (1, 64)))
    key_grad = centred(key_of[7], (LAYERS, KR, HEADS * NOPE), 1.0, 6.0, ((0, 8), (1, 64)))
    return {"logit_partial": logit_partial, "head_order": head_order, "query_weight": query_weight, "query_moment": query_moment, "query_grad": query_grad, "key_weight": key_weight, "key_moment": key_moment, "key_grad": key_grad}


MOMENTUM_DECAY = 0.95
LEARN_RATE = 0.02
WEIGHT_DECAY = 0.1
CLIP_LIMIT = 100.0
NEWTON_FIRST = 3.4445
NEWTON_SECOND = -4.775
NEWTON_THIRD = 2.0315
NORM_EPSILON = 1e-07
HIGHEST = lax.Precision.HIGHEST

def orthogonalize(matrix):
    norms = jnp.sqrt(lax.optimization_barrier(jnp.sum(matrix * matrix, axis=(1, 3), keepdims=True)))
    current = matrix / (norms + NORM_EPSILON)
    for sweep in range(ITERS):
        gram = jnp.einsum('lrhc,lrhd->lhcd', current, current, precision=HIGHEST)
        square = jnp.einsum('lhcd,lhde->lhce', gram, gram, precision=HIGHEST)
        mixed = NEWTON_SECOND * gram + NEWTON_THIRD * square
        current = NEWTON_FIRST * current + jnp.einsum('lrhc,lhcd->lrhd', current, mixed, precision=HIGHEST)
    return current

def apply_step(weight, ortho, scale):
    return weight * (1.0 - LEARN_RATE * WEIGHT_DECAY) - LEARN_RATE * scale * ortho

def head_gamma(partial_value, order):
    rowmax = lax.optimization_barrier(jnp.max(partial_value, axis=0))
    count = order.shape[1]
    onehot = order[:, :, None] == jnp.arange(count, dtype=jnp.int32)[None, None, :]
    logit_max = lax.optimization_barrier(jnp.sum(jnp.where(onehot, rowmax[:, :, None], jnp.zeros_like(rowmax)[:, :, None]), axis=1))
    return jnp.minimum(1.0, CLIP_LIMIT / logit_max)

def clip_query(weight, clip_gamma, nope_cols):
    depth, height, total = weight.shape
    count = clip_gamma.shape[1]
    shaped = weight.reshape(depth, height, count, total // count)
    column = jnp.arange(total // count, dtype=jnp.int32)
    factor = jnp.where(column[None, None, :] < nope_cols, jnp.sqrt(clip_gamma)[:, :, None], clip_gamma[:, :, None])
    return (shaped * factor[:, None]).reshape(depth, height, total)

def clip_key(weight, clip_gamma):
    depth, height, total = weight.shape
    count = clip_gamma.shape[1]
    shaped = weight.reshape(depth, height, count, total // count)
    return (shaped * jnp.sqrt(clip_gamma)[:, None, :, None]).reshape(depth, height, total)

def reference(logit_partial, head_order, query_weight, query_moment, query_grad, key_weight, key_moment, key_grad):
    clip_gamma = head_gamma(logit_partial, head_order)
    query_velocity = (MOMENTUM_DECAY * query_moment.astype(jnp.float32) + query_grad.astype(jnp.float32)).astype(jnp.bfloat16)
    key_velocity = (MOMENTUM_DECAY * key_moment.astype(jnp.float32) + key_grad.astype(jnp.float32)).astype(jnp.bfloat16)
    width = NOPE + ROPE
    query_scale = 0.2 * math.sqrt(max(QR, width))
    key_scale = 0.2 * math.sqrt(max(KR, NOPE))

    def one_layer(pieces):
        query_part, query_base, key_part, key_base = pieces
        query_ortho = orthogonalize(query_part.astype(jnp.float32).reshape(1, QR, HEADS, width))[0].reshape(QR, HEADS * width)
        key_ortho = orthogonalize(key_part.astype(jnp.float32).reshape(1, KR, HEADS, NOPE))[0].reshape(KR, HEADS * NOPE)
        return (apply_step(query_base, query_ortho, query_scale), apply_step(key_base, key_ortho, key_scale))
    query_step, key_step = lax.map(one_layer, (query_velocity, query_weight, key_velocity, key_weight))
    query_final = clip_query(query_step, clip_gamma, NOPE)
    key_final = clip_key(key_step, clip_gamma)
    return (query_final, query_velocity, key_final, key_velocity)
```

```python
import functools
import math

import jax
import jax.numpy as jnp
from jax import lax
from jax.experimental import pallas as pl
from jax.experimental.pallas import tpu as pltpu
from jax.sharding import PartitionSpec as P

QR = 1536
KR = 512
NOPE = 128
ROPE = 64
WIDTH = NOPE + ROPE
ITERS = 5
LANES = 128
ROWS = 48


MOMENTUM_DECAY = 0.95
LEARN_RATE = 0.02
WEIGHT_DECAY = 0.1
CLIP_LIMIT = 100.0
NEWTON_FIRST = 3.4445
NEWTON_SECOND = -4.775
NEWTON_THIRD = 2.0315
NORM_EPSILON = 1e-07
HIGHEST = lax.Precision.HIGHEST
MESH = pl.DeviceIdType.MESH


def gram_of(x):
    return lax.dot_general(x, x, (((0,), (0,)), ((), ())), preferred_element_type=jnp.float32)


def mul(a, b):
    return lax.dot_general(
        a, b, (((1,), (0,)), ((), ())), precision=HIGHEST, preferred_element_type=jnp.float32
    )


def low_dot(x, high, low):
    return jnp.dot(x, high, preferred_element_type=jnp.float32) + jnp.dot(
        x, low, preferred_element_type=jnp.float32
    )


def begin(gram):
    size = gram.shape[0]
    eye = lax.broadcasted_iota(jnp.int32, (size, size), 0) == lax.broadcasted_iota(
        jnp.int32, (size, size), 1
    )
    total = jnp.sum(jnp.where(eye, gram, 0.0))
    inverse = 1.0 / (jnp.sqrt(jnp.full((1, 1), total)) + NORM_EPSILON)
    return gram * inverse * inverse, inverse, jnp.where(eye, 1.0, 0.0)


def newton(gram_q, gram_k):
    aq, iq, eq = begin(gram_q)
    ak, ik, ek = begin(gram_k)
    mq = mk = None
    for sweep in range(ITERS):
        sq, sk = mul(aq, aq), mul(ak, ak)
        pq = NEWTON_FIRST * eq + NEWTON_SECOND * aq + NEWTON_THIRD * sq
        pk = NEWTON_FIRST * ek + NEWTON_SECOND * ak + NEWTON_THIRD * sk
        if sweep == 0:
            mq, mk = pq, pk
        else:
            mq, mk = mul(mq, pq), mul(mk, pk)
        if sweep < ITERS - 1:
            yq, yk = mul(aq, pq), mul(ak, pk)
            aq, ak = mul(yq, pq), mul(yk, pk)
    return mq * iq, mk * ik


def split(m):
    high = m.astype(jnp.bfloat16)
    return high, (m - high.astype(jnp.float32)).astype(jnp.bfloat16)


def half_roll(x):
    return pltpu.roll(x, ROPE, 1)


def body(
    owners,
    n_ctx,
    lp_ref,
    order_ref,
    qw_hbm,
    qm_ref,
    qg_ref,
    kw_hbm,
    km_ref,
    kg_ref,
    qf_ref,
    qv_ref,
    kf_ref,
    kv_ref,
    send,
    recv,
    back,
    home,
    wide,
    gram_q,
    gram_k,
    lsend,
    lrecv,
    gamma,
    root,
    qw_ref,
    kw_ref,
    send_sem,
    recv_sem,
    back_sem,
    home_sem,
    lsend_sem,
    lrecv_sem,
    load_sem,
):
    nx = 4 if owners == 64 else 1
    chips = owners // 2
    nz = chips // nx
    group = 8 if owners == 64 else 4
    groups = owners // group
    pairs = group // 2
    me_c = lax.axis_index("ctx")
    me = lax.axis_index("zero")
    core = lax.rem(me, 2)
    chip = lax.div(me, 2)
    x0, z0 = lax.div(chip, nz), lax.rem(chip, nz)

    def offset(t):
        i = lax.rem(t, nz)
        dz = lax.div(i + 1, 2) * (1 - 2 * lax.rem(i + 1, 2))
        dx = lax.rem(t + lax.div(t, nz), nx)
        return dx, dz

    def chip_to(t):
        dx, dz = offset(t)
        return lax.rem(x0 + dx, nx) * nz + lax.rem(z0 + dz + nz, nz)

    def chip_from(t):
        dx, dz = offset(t)
        return lax.rem(x0 - dx + nx, nx) * nz + lax.rem(z0 - dz + nz, nz)

    def core_at(dc):
        return lax.rem(core + dc, 2)

    load_q = pltpu.make_async_copy(qw_hbm, qw_ref, load_sem.at[0])
    load_k = pltpu.make_async_copy(kw_hbm, kw_ref, load_sem.at[1])
    load_q.start()
    load_k.start()

    barrier = pltpu.get_barrier_semaphore()

    @pl.loop(1, owners)
    def _(i):
        pl.semaphore_signal(
            barrier, inc=1, device_id=(me_c, lax.rem(me + i, owners)), device_id_type=MESH
        )

    @pl.loop(1, n_ctx)
    def _(i):
        pl.semaphore_signal(
            barrier, inc=1, device_id=(lax.rem(me_c + i, n_ctx), me), device_id_type=MESH
        )

    heads = lp_ref.shape[1]
    for layer in range(n_ctx):
        lsend[layer, :, 0:heads] = jnp.broadcast_to(lp_ref[layer : layer + 1, :], (8, heads))
        lsend[layer, :, heads:] = jnp.zeros((8, LANES - heads), jnp.float32)

    lane16 = lax.broadcasted_iota(jnp.int32, (16, LANES), 1) < ROPE
    zero8 = jnp.zeros((8, LANES), jnp.float32)

    def make(t):
        p = chip_to(t)
        qs = pl.ds(pl.multiple_of(p * 384, 128), 384)
        ks = pl.ds(pl.multiple_of(p * 256, 128), 256)
        qv = (
            MOMENTUM_DECAY * qm_ref[:, qs].astype(jnp.float32) + qg_ref[:, qs].astype(jnp.float32)
        ).astype(jnp.bfloat16)
        kv = (
            MOMENTUM_DECAY * km_ref[:, ks].astype(jnp.float32) + kg_ref[:, ks].astype(jnp.float32)
        ).astype(jnp.bfloat16)
        qv_ref[:, qs] = qv
        kv_ref[:, ks] = kv
        qv = qv.astype(jnp.float32)
        kv = kv.astype(jnp.float32)
        middle = qv[:, 128:256]
        turned = half_roll(middle)
        low = jnp.concatenate([middle[16:24], zero8], axis=0)
        low_turned = jnp.concatenate([turned[16:24], zero8], axis=0)
        even = 2 * t + core
        odd = 2 * t + 1 - core
        send[even, 0:32, :] = jnp.concatenate([qv[:, 0:128], kv[:, 0:128]], axis=0).astype(
            jnp.bfloat16
        )
        send[even, 32:48, :] = jnp.where(lane16, middle[0:16], low_turned).astype(jnp.bfloat16)
        send[odd, 0:32, :] = jnp.concatenate([qv[:, 256:384], kv[:, 128:256]], axis=0).astype(
            jnp.bfloat16
        )
        send[odd, 32:48, :] = jnp.where(lane16, turned[0:16], low).astype(jnp.bfloat16)

    def out_copy(t, dc):
        j = 2 * t + dc
        return pltpu.make_async_remote_copy(
            src_ref=send.at[j],
            dst_ref=recv.at[j],
            send_sem=send_sem,
            recv_sem=recv_sem.at[lax.div(j, group)],
            device_id=(me_c, 2 * chip_to(t) + core_at(dc)),
            device_id_type=MESH,
        )

    def back_copy(t, dc):
        j = 2 * t + dc
        return pltpu.make_async_remote_copy(
            src_ref=back.at[j],
            dst_ref=home.at[j],
            send_sem=back_sem,
            recv_sem=home_sem.at[lax.div(j, group)],
            device_id=(me_c, 2 * chip_from(t) + core_at(dc)),
            device_id_type=MESH,
        )

    def span(buffer_out, buffer_in, first, size, out_sem, in_sem):
        return pltpu.make_async_remote_copy(
            src_ref=buffer_out.at[pl.ds(first, size)],
            dst_ref=buffer_in.at[pl.ds(first, size)],
            send_sem=out_sem,
            recv_sem=in_sem,
            device_id=(me_c, me),
            device_id_type=MESH,
        )

    make(0)
    recv[0] = send[0]
    pl.semaphore_wait(barrier, owners - 1 + n_ctx - 1)
    out_copy(0, 1).start()

    @pl.loop(1, chips)
    def _(t):
        make(t)
        out_copy(t, 0).start()
        out_copy(t, 1).start()

    @pl.loop(1, n_ctx)
    def _(i):
        other = lax.rem(me_c + i, n_ctx)
        pltpu.make_async_remote_copy(
            src_ref=lsend.at[other],
            dst_ref=lrecv.at[i],
            send_sem=lsend_sem,
            recv_sem=lrecv_sem,
            device_id=(other, me),
            device_id_type=MESH,
        ).start()

    rows = group * 32
    row = lax.rem(lax.broadcasted_iota(jnp.int32, (rows, LANES), 0), 32)
    is_query = row < 24
    lane = lax.broadcasted_iota(jnp.int32, (group * 16, LANES), 1) < ROPE

    def gather(k):
        first = pl.multiple_of(k * rows, rows)
        block = recv[pl.ds(k * group, group), 0:32, :].reshape(rows, LANES).astype(jnp.float32)
        third = recv[pl.ds(k * group, group), 32:48, :].reshape(group * 16, LANES)
        third = third.astype(jnp.float32)
        top = jnp.where(lane, third, 0.0).reshape(group, 16, LANES)
        bottom = jnp.where(lane, half_roll(third), 0.0).reshape(group, 16, LANES)
        third = jnp.concatenate([top, bottom], axis=1).reshape(rows, LANES)
        query = jnp.where(is_query, block, 0.0).astype(jnp.bfloat16)
        key = jnp.where(is_query, 0.0, block).astype(jnp.bfloat16)
        full = jnp.concatenate([query, third.astype(jnp.bfloat16)], axis=1)
        wide[pl.ds(first, rows), 0:256] = full
        wide[pl.ds(first, rows), 256:384] = key
        gram_q[...] += gram_of(full)
        gram_k[...] += gram_of(key)

    gram_q[...] = jnp.zeros_like(gram_q)
    gram_k[...] = jnp.zeros_like(gram_k)
    span(send, recv, 1, group - 1, send_sem, recv_sem.at[0]).wait_recv()
    gather(0)

    @pl.loop(1, groups)
    def _(k):
        span(send, recv, k * group, group, send_sem, recv_sem.at[k]).wait_recv()
        gather(k)

    mq, mk = newton(gram_q[...], gram_k[...])
    mq_high, mq_low = split(mq)
    mk_high, mk_low = split(mk)

    def give(k):
        first = pl.multiple_of(k * rows, rows)
        query = low_dot(wide[pl.ds(first, rows), 0:256], mq_high, mq_low)
        key = low_dot(wide[pl.ds(first, rows), 256:384], mk_high, mk_low)
        block = query[:, 0:128] + key
        third = query[:, 128:256].reshape(group, 32, LANES)
        top = third[:, 0:16].reshape(group * 16, LANES)
        bottom = half_roll(third[:, 16:32].reshape(group * 16, LANES))
        third = jnp.where(lane, top, bottom)
        back[pl.ds(k * group, group), 0:32, :] = block.astype(jnp.bfloat16).reshape(
            group, 32, LANES
        )
        back[pl.ds(k * group, group), 32:48, :] = third.astype(jnp.bfloat16).reshape(
            group, 16, LANES
        )

    give(0)
    back_copy(0, 1).start()
    for t in range(1, pairs):
        back_copy(t, 0).start()
        back_copy(t, 1).start()
    home[0] = back[0]

    @pl.loop(1, groups)
    def _(k):
        give(k)

        @pl.loop(0, pairs)
        def _(i):
            back_copy(k * pairs + i, 0).start()
            back_copy(k * pairs + i, 1).start()

    lrecv[0] = lsend[me_c]
    pltpu.make_async_remote_copy(
        src_ref=lsend.at[pl.ds(1, n_ctx - 1)],
        dst_ref=lrecv.at[pl.ds(1, n_ctx - 1)],
        send_sem=lsend_sem,
        recv_sem=lrecv_sem,
        device_id=(me_c, me),
        device_id_type=MESH,
    ).wait()
    rowmax = jnp.max(lrecv[...], axis=0)[0:1, 0:heads]
    order = order_ref[pl.ds(me_c, 1), :]
    hit = jnp.broadcast_to(order, (heads, heads)) == lax.broadcasted_iota(
        jnp.int32, (heads, heads), 0
    )
    logit_max = jnp.sum(
        jnp.where(hit, jnp.broadcast_to(rowmax, (heads, heads)), 0.0), axis=1, keepdims=True
    )
    clip = jnp.minimum(1.0, CLIP_LIMIT / logit_max)
    gamma[...] = jnp.broadcast_to(clip, (heads, LANES))
    root[...] = jnp.broadcast_to(jnp.sqrt(clip), (heads, LANES))

    load_q.wait()
    load_k.wait()
    keep = 1.0 - LEARN_RATE * WEIGHT_DECAY
    rate_q = LEARN_RATE * (0.2 * math.sqrt(max(QR, WIDTH)))
    rate_k = LEARN_RATE * (0.2 * math.sqrt(max(KR, NOPE)))
    lane1 = lax.broadcasted_iota(jnp.int32, (1, LANES), 1) < ROPE

    def finish(t):
        p = chip_to(t)
        even = home[2 * t + core].astype(jnp.float32)
        odd = home[2 * t + 1 - core].astype(jnp.float32)
        even_third, odd_third = even[32:48], odd[32:48]
        even_turned, odd_turned = half_roll(even_third), half_roll(odd_third)
        middle = jnp.concatenate(
            [
                jnp.where(lane16, even_third, odd_turned),
                jnp.where(lane16, even_turned, odd_third)[0:8],
            ],
            axis=0,
        )
        g_even, g_odd = gamma[pl.ds(2 * p, 1), :], gamma[pl.ds(2 * p + 1, 1), :]
        r_even, r_odd = root[pl.ds(2 * p, 1), :], root[pl.ds(2 * p + 1, 1), :]
        tiles = (
            (even[0:24], r_even),
            (middle, jnp.where(lane1, g_even, r_odd)),
            (odd[0:24], jnp.where(lane1, r_odd, g_odd)),
        )
        for i, (ortho, factor) in enumerate(tiles):
            at = pl.ds(pl.multiple_of(p * 384 + i * 128, 128), 128)
            qf_ref[:, at] = (qw_ref[:, at] * keep - rate_q * ortho) * factor
        for i, (ortho, factor) in enumerate(((even[24:32], r_even), (odd[24:32], r_odd))):
            at = pl.ds(pl.multiple_of(p * 256 + i * 128, 128), 128)
            kf_ref[:, at] = (kw_ref[:, at] * keep - rate_k * ortho) * factor

    span(back, home, 1, group - 1, back_sem, home_sem.at[0]).wait_recv()

    @pl.loop(0, pairs)
    def _(i):
        finish(i)

    @pl.loop(1, groups)
    def _(k):
        span(back, home, k * group, group, back_sem, home_sem.at[k]).wait_recv()

        @pl.loop(0, pairs)
        def _(i):
            finish(k * pairs + i)

    span(send, recv, 1, owners - 1, send_sem, recv_sem.at[0]).wait_send()
    span(back, home, 1, owners - 1, back_sem, home_sem.at[0]).wait_send()


def local(
    logit_partial,
    head_order,
    query_weight,
    query_moment,
    query_grad,
    key_weight,
    key_moment,
    key_grad,
):
    owners = lax.axis_size("zero")
    n_ctx = lax.axis_size("ctx")
    groups = owners // (8 if owners == 64 else 4)
    heads = head_order.shape[1]
    query, key = query_weight.shape[1:], key_weight.shape[1:]
    vmem = pl.BlockSpec(memory_space=pltpu.VMEM)
    hbm = pl.BlockSpec(memory_space=pl.ANY)
    dma = pltpu.SemaphoreType.DMA
    qf, qv, kf, kv = pl.pallas_call(
        functools.partial(body, owners, n_ctx),
        out_shape=(
            jax.ShapeDtypeStruct(query, jnp.float32),
            jax.ShapeDtypeStruct(query, jnp.bfloat16),
            jax.ShapeDtypeStruct(key, jnp.float32),
            jax.ShapeDtypeStruct(key, jnp.bfloat16),
        ),
        in_specs=[vmem, vmem, hbm, vmem, vmem, hbm, vmem, vmem],
        out_specs=(vmem, vmem, vmem, vmem),
        scratch_shapes=[
            pltpu.VMEM((owners, ROWS, LANES), jnp.bfloat16),
            pltpu.VMEM((owners, ROWS, LANES), jnp.bfloat16),
            pltpu.VMEM((owners, ROWS, LANES), jnp.bfloat16),
            pltpu.VMEM((owners, ROWS, LANES), jnp.bfloat16),
            pltpu.VMEM((owners * 32, 384), jnp.bfloat16),
            pltpu.VMEM((256, 256), jnp.float32),
            pltpu.VMEM((128, 128), jnp.float32),
            pltpu.VMEM((n_ctx, 8, LANES), jnp.float32),
            pltpu.VMEM((n_ctx, 8, LANES), jnp.float32),
            pltpu.VMEM((heads, LANES), jnp.float32),
            pltpu.VMEM((heads, LANES), jnp.float32),
            pltpu.VMEM(query, jnp.float32),
            pltpu.VMEM(key, jnp.float32),
            dma,
            dma((groups,)),
            dma,
            dma((groups,)),
            dma,
            dma,
            dma((2,)),
        ],
        compiler_params=pltpu.CompilerParams(
            collective_id=0, has_side_effects=True, vmem_limit_bytes=48 * 1024 * 1024
        ),
        name="muon",
    )(
        logit_partial[0],
        head_order,
        query_weight[0],
        query_moment[0],
        query_grad[0],
        key_weight[0],
        key_moment[0],
        key_grad[0],
    )
    return (qf[None], qv[None], kf[None], kv[None])


def solution(mesh):
    shard = P("ctx", "zero", None)
    return jax.shard_map(
        local,
        mesh=mesh,
        in_specs=(P("ctx", None, None), P(), shard, shard, shard, shard, shard, shard),
        out_specs=(shard, shard, shard, shard),
        check_vma=False,
    )
```

```python
import functools
import math

import jax
import jax.numpy as jnp
from jax import lax
from jax.experimental import pallas as pl
from jax.experimental.pallas import tpu as pltpu
from jax.sharding import PartitionSpec as P

QR = 1536
KR = 512
NOPE = 128
ROPE = 64
WIDTH = NOPE + ROPE
ITERS = 5
LANES = 128
ROWS = 48


MOMENTUM_DECAY = 0.95
LEARN_RATE = 0.02
WEIGHT_DECAY = 0.1
CLIP_LIMIT = 100.0
NEWTON_FIRST = 3.4445
NEWTON_SECOND = -4.775
NEWTON_THIRD = 2.0315
NORM_EPSILON = 1e-07
HIGHEST = lax.Precision.HIGHEST
MESH = pl.DeviceIdType.MESH


def gram_of(x):
    return lax.dot_general(x, x, (((0,), (0,)), ((), ())), preferred_element_type=jnp.float32)


def mul(a, b):
    return lax.dot_general(
        a, b, (((1,), (0,)), ((), ())), precision=HIGHEST, preferred_element_type=jnp.float32
    )


def low_dot(x, high, low):
    return jnp.dot(x, high, preferred_element_type=jnp.float32) + jnp.dot(
        x, low, preferred_element_type=jnp.float32
    )


def begin(gram, size):
    gram = gram[0:size]
    eye = lax.broadcasted_iota(jnp.int32, gram.shape, 0) == lax.broadcasted_iota(
        jnp.int32, gram.shape, 1
    )
    total = jnp.sum(jnp.where(eye, gram, 0.0), axis=1, keepdims=True)
    total = jnp.sum(total, axis=0, keepdims=True)
    inverse = 1.0 / (jnp.sqrt(total) + NORM_EPSILON)
    return gram * inverse * inverse, inverse, jnp.where(eye, 1.0, 0.0)


def square(x):
    missing = x.shape[1] - x.shape[0]
    if not missing:
        return x
    return jnp.concatenate([x, jnp.zeros((missing, x.shape[1]), x.dtype)], axis=0)


def split(m):
    high = m.astype(jnp.bfloat16)
    return high, (m - high.astype(jnp.float32)).astype(jnp.bfloat16)


def mul3(a, b):
    b_high, b_low = square(b[0]), square(b[1])
    return (
        jnp.dot(a[0], b_high, preferred_element_type=jnp.float32)
        + jnp.dot(a[0], b_low, preferred_element_type=jnp.float32)
        + jnp.dot(a[1], b_high, preferred_element_type=jnp.float32)
    )


def stack(a, b):
    return tuple(jnp.concatenate(pair, axis=0) for pair in zip(a, b))


def newton(grams):
    a, inverse, eye = (list(x) for x in zip(*grams))
    m = [None] * len(a)
    which = range(len(a))
    for sweep in range(ITERS):
        exact = sweep == 0
        halves = [split(a[i]) for i in which]
        if exact:
            s = [mul(a[i], square(a[i])) for i in which]
        else:
            s = [mul3(halves[i], halves[i]) for i in which]
        p = [NEWTON_FIRST * eye[i] + NEWTON_SECOND * a[i] + NEWTON_THIRD * s[i] for i in which]
        p_halves = [split(p[i]) for i in which]
        if exact:
            y = [mul(a[i], square(p[i])) for i in which]
            a = [mul(y[i], square(p[i])) for i in which]
            m = p
        elif sweep < ITERS - 1:
            both = [mul3(stack(halves[i], split(m[i])), p_halves[i]) for i in which]
            size = [a[i].shape[0] for i in which]
            a = [mul3(split(both[i][0 : size[i]]), p_halves[i]) for i in which]
            m = [both[i][size[i] :] for i in which]
        else:
            m = [mul3(split(m[i]), p_halves[i]) for i in which]
    return [m[i] * inverse[i] for i in which]


def half_roll(x):
    return pltpu.roll(x, ROPE, 1)


def body(
    owners,
    n_ctx,
    lp_hbm,
    order_hbm,
    qw_hbm,
    qm_hbm,
    qg_hbm,
    kw_hbm,
    km_hbm,
    kg_hbm,
    qf_ref,
    qv_ref,
    kf_ref,
    kv_ref,
    send,
    recv,
    back,
    home,
    wide,
    gram_q,
    gram_k,
    lsend,
    lrecv,
    gamma,
    root,
    qw_ref,
    kw_ref,
    qm_ref,
    qg_ref,
    km_ref,
    kg_ref,
    lp_ref,
    order_ref,
    send_sem,
    recv_sem,
    back_sem,
    home_sem,
    lsend_sem,
    lrecv_sem,
    load_sem,
):
    nx = 4 if owners == 64 else 1
    chips = owners // 2
    nz = chips // nx
    group = 8 if owners == 64 else 4
    groups = owners // group
    pairs = group // 2
    me_c = lax.axis_index("ctx")
    me = lax.axis_index("zero")
    core = lax.rem(me, 2)
    chip = lax.div(me, 2)
    x0, z0 = lax.div(chip, nz), lax.rem(chip, nz)

    def offset(t):
        i = lax.rem(t, nz)
        dz = lax.div(i + 1, 2) * (1 - 2 * lax.rem(i + 1, 2))
        dx = lax.rem(t + lax.div(t, nz), nx)
        return dx, dz

    def chip_to(t):
        dx, dz = offset(t)
        return lax.rem(x0 + dx, nx) * nz + lax.rem(z0 + dz + nz, nz)

    def chip_from(t):
        dx, dz = offset(t)
        return lax.rem(x0 - dx + nx, nx) * nz + lax.rem(z0 - dz + nz, nz)

    def core_at(dc):
        return lax.rem(core + dc, 2)

    loads = [
        pltpu.make_async_copy(source, target, load_sem.at[i])
        for i, (source, target) in enumerate(
            (
                (qm_hbm, qm_ref),
                (qg_hbm, qg_ref),
                (km_hbm, km_ref),
                (kg_hbm, kg_ref),
                (lp_hbm, lp_ref),
                (order_hbm, order_ref),
                (qw_hbm, qw_ref),
                (kw_hbm, kw_ref),
            )
        )
    ]
    for load in loads:
        load.start()

    barrier = pltpu.get_barrier_semaphore()

    @pl.loop(1, owners)
    def _(i):
        pl.semaphore_signal(
            barrier, inc=1, device_id=(me_c, lax.rem(me + i, owners)), device_id_type=MESH
        )

    @pl.loop(1, n_ctx)
    def _(i):
        pl.semaphore_signal(
            barrier, inc=1, device_id=(lax.rem(me_c + i, n_ctx), me), device_id_type=MESH
        )

    heads = lp_ref.shape[1]
    for load in loads[:5]:
        load.wait()
    for layer in range(n_ctx):
        lsend[layer, :, 0:heads] = jnp.broadcast_to(lp_ref[layer : layer + 1, :], (8, heads))
        lsend[layer, :, heads:] = jnp.zeros((8, LANES - heads), jnp.float32)

    lane16 = lax.broadcasted_iota(jnp.int32, (16, LANES), 1) < ROPE
    zero8 = jnp.zeros((8, LANES), jnp.float32)

    def make(t):
        p = chip_to(t)
        qs = pl.ds(pl.multiple_of(p * 384, 128), 384)
        ks = pl.ds(pl.multiple_of(p * 256, 128), 256)
        qv = (
            MOMENTUM_DECAY * qm_ref[:, qs].astype(jnp.float32) + qg_ref[:, qs].astype(jnp.float32)
        ).astype(jnp.bfloat16)
        kv = (
            MOMENTUM_DECAY * km_ref[:, ks].astype(jnp.float32) + kg_ref[:, ks].astype(jnp.float32)
        ).astype(jnp.bfloat16)
        qv_ref[:, qs] = qv
        kv_ref[:, ks] = kv
        qv = qv.astype(jnp.float32)
        kv = kv.astype(jnp.float32)
        middle = qv[:, 128:256]
        turned = half_roll(middle)
        low = jnp.concatenate([middle[16:24], zero8], axis=0)
        low_turned = jnp.concatenate([turned[16:24], zero8], axis=0)
        even = 2 * t + core
        odd = 2 * t + 1 - core
        send[even, 0:32, :] = jnp.concatenate([qv[:, 0:128], kv[:, 0:128]], axis=0).astype(
            jnp.bfloat16
        )
        send[even, 32:48, :] = jnp.where(lane16, middle[0:16], low_turned).astype(jnp.bfloat16)
        send[odd, 0:32, :] = jnp.concatenate([qv[:, 256:384], kv[:, 128:256]], axis=0).astype(
            jnp.bfloat16
        )
        send[odd, 32:48, :] = jnp.where(lane16, turned[0:16], low).astype(jnp.bfloat16)

    def out_copy(t, dc):
        j = 2 * t + dc
        return pltpu.make_async_remote_copy(
            src_ref=send.at[j],
            dst_ref=recv.at[j],
            send_sem=send_sem,
            recv_sem=recv_sem.at[lax.div(j, group)],
            device_id=(me_c, 2 * chip_to(t) + core_at(dc)),
            device_id_type=MESH,
        )

    def back_copy(t, dc):
        j = 2 * t + dc
        return pltpu.make_async_remote_copy(
            src_ref=back.at[j],
            dst_ref=home.at[j],
            send_sem=back_sem,
            recv_sem=home_sem.at[lax.div(j, group)],
            device_id=(me_c, 2 * chip_from(t) + core_at(dc)),
            device_id_type=MESH,
        )

    def span(buffer_out, buffer_in, first, size, out_sem, in_sem):
        return pltpu.make_async_remote_copy(
            src_ref=buffer_out.at[pl.ds(first, size)],
            dst_ref=buffer_in.at[pl.ds(first, size)],
            send_sem=out_sem,
            recv_sem=in_sem,
            device_id=(me_c, me),
            device_id_type=MESH,
        )

    make(0)
    recv[0] = send[0]
    pl.semaphore_wait(barrier, owners - 1 + n_ctx - 1)
    out_copy(0, 1).start()

    @pl.loop(1, chips)
    def _(t):
        make(t)
        out_copy(t, 0).start()
        out_copy(t, 1).start()

    @pl.loop(1, n_ctx)
    def _(i):
        other = lax.rem(me_c + i, n_ctx)
        pltpu.make_async_remote_copy(
            src_ref=lsend.at[other],
            dst_ref=lrecv.at[i],
            send_sem=lsend_sem,
            recv_sem=lrecv_sem,
            device_id=(other, me),
            device_id_type=MESH,
        ).start()

    rows = group * 32
    row = lax.rem(lax.broadcasted_iota(jnp.int32, (rows, LANES), 0), 32)
    is_query = row < 24
    lane = lax.broadcasted_iota(jnp.int32, (group * 16, LANES), 1) < ROPE

    def gather(k):
        first = pl.multiple_of(k * rows, rows)
        block = recv[pl.ds(k * group, group), 0:32, :].reshape(rows, LANES).astype(jnp.float32)
        third = recv[pl.ds(k * group, group), 32:48, :].reshape(group * 16, LANES)
        third = third.astype(jnp.float32)
        top = jnp.where(lane, third, 0.0).reshape(group, 16, LANES)
        bottom = jnp.where(lane, half_roll(third), 0.0).reshape(group, 16, LANES)
        third = jnp.concatenate([top, bottom], axis=1).reshape(rows, LANES)
        query = jnp.where(is_query, block, 0.0).astype(jnp.bfloat16)
        key = jnp.where(is_query, 0.0, block).astype(jnp.bfloat16)
        full = jnp.concatenate([query, third.astype(jnp.bfloat16)], axis=1)
        wide[pl.ds(first, rows), 0:256] = full
        wide[pl.ds(first, rows), 256:384] = key
        gram_q[...] += gram_of(full)
        gram_k[...] += gram_of(key)

    gram_q[...] = jnp.zeros_like(gram_q)
    gram_k[...] = jnp.zeros_like(gram_k)
    span(send, recv, 1, group - 1, send_sem, recv_sem.at[0]).wait_recv()
    gather(0)

    @pl.loop(1, groups)
    def _(k):
        span(send, recv, k * group, group, send_sem, recv_sem.at[k]).wait_recv()
        gather(k)

    mq, mk = newton([begin(gram_q[...], WIDTH), begin(gram_k[...], NOPE)])
    mq_high, mq_low = split(square(mq))
    mk_high, mk_low = split(mk)

    def give(k):
        first = pl.multiple_of(k * rows, rows)
        query = low_dot(wide[pl.ds(first, rows), 0:256], mq_high, mq_low)
        key = low_dot(wide[pl.ds(first, rows), 256:384], mk_high, mk_low)
        block = query[:, 0:128] + key
        third = query[:, 128:256].reshape(group, 32, LANES)
        top = third[:, 0:16].reshape(group * 16, LANES)
        bottom = half_roll(third[:, 16:32].reshape(group * 16, LANES))
        third = jnp.where(lane, top, bottom)
        back[pl.ds(k * group, group), 0:32, :] = block.astype(jnp.bfloat16).reshape(
            group, 32, LANES
        )
        back[pl.ds(k * group, group), 32:48, :] = third.astype(jnp.bfloat16).reshape(
            group, 16, LANES
        )

    give(0)
    back_copy(0, 1).start()
    for t in range(1, pairs):
        back_copy(t, 0).start()
        back_copy(t, 1).start()
    home[0] = back[0]

    @pl.loop(1, groups)
    def _(k):
        give(k)

        @pl.loop(0, pairs)
        def _(i):
            back_copy(k * pairs + i, 0).start()
            back_copy(k * pairs + i, 1).start()

    lrecv[0] = lsend[me_c]
    pltpu.make_async_remote_copy(
        src_ref=lsend.at[pl.ds(1, n_ctx - 1)],
        dst_ref=lrecv.at[pl.ds(1, n_ctx - 1)],
        send_sem=lsend_sem,
        recv_sem=lrecv_sem,
        device_id=(me_c, me),
        device_id_type=MESH,
    ).wait()
    rowmax = jnp.max(lrecv[...], axis=0)[0:1, 0:heads]
    loads[5].wait()
    order = order_ref[pl.ds(me_c, 1), :]
    hit = jnp.broadcast_to(order, (heads, heads)) == lax.broadcasted_iota(
        jnp.int32, (heads, heads), 0
    )
    logit_max = jnp.sum(
        jnp.where(hit, jnp.broadcast_to(rowmax, (heads, heads)), 0.0), axis=1, keepdims=True
    )
    clip = jnp.minimum(1.0, CLIP_LIMIT / logit_max)
    gamma[...] = jnp.broadcast_to(clip, (heads, LANES))
    root[...] = jnp.broadcast_to(jnp.sqrt(clip), (heads, LANES))

    for load in loads[6:]:
        load.wait()
    keep = 1.0 - LEARN_RATE * WEIGHT_DECAY
    rate_q = LEARN_RATE * (0.2 * math.sqrt(max(QR, WIDTH)))
    rate_k = LEARN_RATE * (0.2 * math.sqrt(max(KR, NOPE)))
    lane1 = lax.broadcasted_iota(jnp.int32, (1, LANES), 1) < ROPE

    def finish(t):
        p = chip_to(t)
        even = home[2 * t + core].astype(jnp.float32)
        odd = home[2 * t + 1 - core].astype(jnp.float32)
        even_third, odd_third = even[32:48], odd[32:48]
        even_turned, odd_turned = half_roll(even_third), half_roll(odd_third)
        middle = jnp.concatenate(
            [
                jnp.where(lane16, even_third, odd_turned),
                jnp.where(lane16, even_turned, odd_third)[0:8],
            ],
            axis=0,
        )
        g_even, g_odd = gamma[pl.ds(2 * p, 1), :], gamma[pl.ds(2 * p + 1, 1), :]
        r_even, r_odd = root[pl.ds(2 * p, 1), :], root[pl.ds(2 * p + 1, 1), :]
        tiles = (
            (even[0:24], r_even),
            (middle, jnp.where(lane1, g_even, r_odd)),
            (odd[0:24], jnp.where(lane1, r_odd, g_odd)),
        )
        done = []
        for i, (ortho, factor) in enumerate(tiles):
            at = pl.ds(pl.multiple_of(p * 384 + i * 128, 128), 128)
            done.append((qf_ref, at, (qw_ref[:, at] * keep - rate_q * ortho) * factor))
        for i, (ortho, factor) in enumerate(((even[24:32], r_even), (odd[24:32], r_odd))):
            at = pl.ds(pl.multiple_of(p * 256 + i * 128, 128), 128)
            done.append((kf_ref, at, (kw_ref[:, at] * keep - rate_k * ortho) * factor))
        return done

    def finish_group(k):
        done = []
        for i in range(pairs):
            done += finish(k * pairs + i)
        for ref, at, value in done:
            ref[:, at] = value

    span(back, home, 1, group - 1, back_sem, home_sem.at[0]).wait_recv()
    finish_group(0)

    @pl.loop(1, groups)
    def _(k):
        span(back, home, k * group, group, back_sem, home_sem.at[k]).wait_recv()
        finish_group(k)

    span(send, recv, 1, owners - 1, send_sem, recv_sem.at[0]).wait_send()
    span(back, home, 1, owners - 1, back_sem, home_sem.at[0]).wait_send()


def emit(*refs):
    sem = refs[8]
    copies = [pltpu.make_async_copy(refs[i], refs[4 + i], sem.at[i]) for i in range(4)]
    for copy in copies:
        copy.start()
    for copy in copies:
        copy.wait()


def local(
    logit_partial,
    head_order,
    query_weight,
    query_moment,
    query_grad,
    key_weight,
    key_moment,
    key_grad,
):
    owners = lax.axis_size("zero")
    n_ctx = lax.axis_size("ctx")
    groups = owners // (8 if owners == 64 else 4)
    heads = head_order.shape[1]
    query, key = query_weight.shape[1:], key_weight.shape[1:]
    vmem = pl.BlockSpec(memory_space=pltpu.VMEM)
    hbm = pl.BlockSpec(memory_space=pltpu.HBM)
    dma = pltpu.SemaphoreType.DMA
    shapes = (
        jax.ShapeDtypeStruct(query, jnp.float32),
        jax.ShapeDtypeStruct(query, jnp.bfloat16),
        jax.ShapeDtypeStruct(key, jnp.float32),
        jax.ShapeDtypeStruct(key, jnp.bfloat16),
    )
    results = pl.pallas_call(
        functools.partial(body, owners, n_ctx),
        out_shape=shapes,
        in_specs=[hbm] * 8,
        out_specs=(vmem, vmem, vmem, vmem),
        scratch_shapes=[
            pltpu.VMEM((owners, ROWS, LANES), jnp.bfloat16),
            pltpu.VMEM((owners, ROWS, LANES), jnp.bfloat16),
            pltpu.VMEM((owners, ROWS, LANES), jnp.bfloat16),
            pltpu.VMEM((owners, ROWS, LANES), jnp.bfloat16),
            pltpu.VMEM((owners * 32, 384), jnp.bfloat16),
            pltpu.VMEM((256, 256), jnp.float32),
            pltpu.VMEM((128, 128), jnp.float32),
            pltpu.VMEM((n_ctx, 8, LANES), jnp.float32),
            pltpu.VMEM((n_ctx, 8, LANES), jnp.float32),
            pltpu.VMEM((heads, LANES), jnp.float32),
            pltpu.VMEM((heads, LANES), jnp.float32),
            pltpu.VMEM(query, jnp.float32),
            pltpu.VMEM(key, jnp.float32),
            pltpu.VMEM(query, jnp.bfloat16),
            pltpu.VMEM(query, jnp.bfloat16),
            pltpu.VMEM(key, jnp.bfloat16),
            pltpu.VMEM(key, jnp.bfloat16),
            pltpu.VMEM(logit_partial.shape[1:], jnp.float32),
            pltpu.VMEM(head_order.shape, jnp.int32),
            dma,
            dma((groups,)),
            dma,
            dma((groups,)),
            dma,
            dma,
            dma((8,)),
        ],
        compiler_params=pltpu.CompilerParams(
            collective_id=0, has_side_effects=True, vmem_limit_bytes=48 * 1024 * 1024
        ),
        name="muon",
    )(
        *(
            pltpu.with_memory_space_constraint(array, pltpu.HBM)
            for array in (
                logit_partial[0],
                head_order,
                query_weight[0],
                query_moment[0],
                query_grad[0],
                key_weight[0],
                key_moment[0],
                key_grad[0],
            )
        )
    )
    results = pl.pallas_call(
        emit,
        out_shape=shapes,
        in_specs=[vmem] * 4,
        out_specs=[hbm] * 4,
        scratch_shapes=[dma((4,))],
        name="emit",
    )(*results)
    return tuple(result[None] for result in results)


def solution(mesh):
    shard = P("ctx", "zero", None)
    return jax.shard_map(
        local,
        mesh=mesh,
        in_specs=(P("ctx", None, None), P(), shard, shard, shard, shard, shard, shard),
        out_specs=(shard, shard, shard, shard),
        check_vma=False,
    )
```

```python
import functools
import math

import jax
import jax.numpy as jnp
from jax import lax
from jax.experimental import pallas as pl
from jax.experimental.pallas import tpu as pltpu
from jax.sharding import PartitionSpec as P

QR = 1536
KR = 512
NOPE = 128
ROPE = 64
WIDTH = NOPE + ROPE
ITERS = 5
LANES = 128
ROWS = 48


MOMENTUM_DECAY = 0.95
LEARN_RATE = 0.02
WEIGHT_DECAY = 0.1
CLIP_LIMIT = 100.0
NEWTON_FIRST = 3.4445
NEWTON_SECOND = -4.775
NEWTON_THIRD = 2.0315
NORM_EPSILON = 1e-07
HIGHEST = lax.Precision.HIGHEST
MESH = pl.DeviceIdType.MESH


def gram_of(x):
    return lax.dot_general(x, x, (((0,), (0,)), ((), ())), preferred_element_type=jnp.float32)


def mul(a, b):
    return lax.dot_general(
        a, b, (((1,), (0,)), ((), ())), precision=HIGHEST, preferred_element_type=jnp.float32
    )


def low_dot(x, high, low):
    return jnp.dot(x, high, preferred_element_type=jnp.float32) + jnp.dot(
        x, low, preferred_element_type=jnp.float32
    )


def begin(gram, size):
    gram = gram[0:size]
    eye = lax.broadcasted_iota(jnp.int32, gram.shape, 0) == lax.broadcasted_iota(
        jnp.int32, gram.shape, 1
    )
    total = jnp.sum(jnp.where(eye, gram, 0.0), axis=1, keepdims=True)
    total = jnp.sum(total, axis=0, keepdims=True)
    inverse = 1.0 / (jnp.sqrt(total) + NORM_EPSILON)
    return gram * inverse * inverse, inverse, jnp.where(eye, 1.0, 0.0)


def square(x):
    missing = x.shape[1] - x.shape[0]
    if not missing:
        return x
    return jnp.concatenate([x, jnp.zeros((missing, x.shape[1]), x.dtype)], axis=0)


def split(m):
    high = m.astype(jnp.bfloat16)
    return high, (m - high.astype(jnp.float32)).astype(jnp.bfloat16)


def mul3(a, b):
    b_high, b_low = square(b[0]), square(b[1])
    return (
        jnp.dot(a[0], b_high, preferred_element_type=jnp.float32)
        + jnp.dot(a[0], b_low, preferred_element_type=jnp.float32)
        + jnp.dot(a[1], b_high, preferred_element_type=jnp.float32)
    )


def stack(a, b):
    return tuple(jnp.concatenate(pair, axis=0) for pair in zip(a, b))


def newton(grams):
    a, inverse, eye = (list(x) for x in zip(*grams))
    m = [None] * len(a)
    which = range(len(a))
    for sweep in range(ITERS):
        exact = sweep == 0
        halves = [split(a[i]) for i in which]
        if exact:
            s = [mul(a[i], square(a[i])) for i in which]
        else:
            s = [mul3(halves[i], halves[i]) for i in which]
        p = [NEWTON_FIRST * eye[i] + NEWTON_SECOND * a[i] + NEWTON_THIRD * s[i] for i in which]
        p_halves = [split(p[i]) for i in which]
        if exact:
            y = [mul(a[i], square(p[i])) for i in which]
            a = [mul(y[i], square(p[i])) for i in which]
            m = p
        elif sweep < ITERS - 1:
            both = [mul3(stack(halves[i], split(m[i])), p_halves[i]) for i in which]
            size = [a[i].shape[0] for i in which]
            a = [mul3(split(both[i][0 : size[i]]), p_halves[i]) for i in which]
            m = [both[i][size[i] :] for i in which]
        else:
            m = [mul3(split(m[i]), p_halves[i]) for i in which]
    return [m[i] * inverse[i] for i in which]


def half_roll(x):
    return pltpu.roll(x, ROPE, 1)


def body(
    owners,
    n_ctx,
    lp_hbm,
    order_hbm,
    qw_hbm,
    qm_hbm,
    qg_hbm,
    kw_hbm,
    km_hbm,
    kg_hbm,
    qf_ref,
    qv_ref,
    kf_ref,
    kv_ref,
    send,
    recv,
    back,
    home,
    relay,
    relay_back,
    wide,
    gram_q,
    gram_k,
    lsend,
    lrecv,
    gamma,
    root,
    qw_ref,
    kw_ref,
    qm_ref,
    qg_ref,
    km_ref,
    kg_ref,
    lp_ref,
    order_ref,
    send_sem,
    recv_sem,
    back_sem,
    home_sem,
    relay_sem,
    lsend_sem,
    lrecv_sem,
    load_sem,
):
    nx = 4 if owners == 64 else 1
    chips = owners // 2
    nz = chips // nx
    group = 2 * nx
    groups = owners // group
    pairs = group // 2
    direct = nx * (nz - 1)
    quarter = nz // 4
    me_c = lax.axis_index("ctx")
    me = lax.axis_index("zero")
    core = lax.rem(me, 2)
    chip = lax.div(me, 2)
    x0, z0 = lax.div(chip, nz), lax.rem(chip, nz)

    def offset(t):
        if isinstance(t, int) and t >= direct:
            return t - direct, 2 * quarter
        i = lax.rem(t, nz - 1)
        dz = lax.div(i + 1, 2) * (1 - 2 * lax.rem(i + 1, 2))
        dx = lax.rem(i + lax.div(t, nz - 1), nx)
        return dx, dz

    def chip_to(t):
        dx, dz = offset(t)
        return lax.rem(x0 + dx, nx) * nz + lax.rem(z0 + dz + nz, nz)

    def chip_from(t):
        dx, dz = offset(t)
        return lax.rem(x0 - dx + nx, nx) * nz + lax.rem(z0 - dz + nz, nz)

    def core_at(dc):
        return lax.rem(core + dc, 2)

    loads = [
        pltpu.make_async_copy(source, target, load_sem.at[i])
        for i, (source, target) in enumerate(
            (
                (qm_hbm, qm_ref),
                (qg_hbm, qg_ref),
                (km_hbm, km_ref),
                (kg_hbm, kg_ref),
                (lp_hbm, lp_ref),
                (order_hbm, order_ref),
                (qw_hbm, qw_ref),
                (kw_hbm, kw_ref),
            )
        )
    ]
    for load in loads:
        load.start()

    barrier = pltpu.get_barrier_semaphore()

    @pl.loop(1, owners)
    def _(i):
        pl.semaphore_signal(
            barrier, inc=1, device_id=(me_c, lax.rem(me + i, owners)), device_id_type=MESH
        )

    @pl.loop(1, n_ctx)
    def _(i):
        pl.semaphore_signal(
            barrier, inc=1, device_id=(lax.rem(me_c + i, n_ctx), me), device_id_type=MESH
        )

    heads = lp_ref.shape[1]
    for load in loads[:5]:
        load.wait()
    for layer in range(n_ctx):
        lsend[layer, :, 0:heads] = jnp.broadcast_to(lp_ref[layer : layer + 1, :], (8, heads))
        lsend[layer, :, heads:] = jnp.zeros((8, LANES - heads), jnp.float32)

    lane16 = lax.broadcasted_iota(jnp.int32, (16, LANES), 1) < ROPE
    zero8 = jnp.zeros((8, LANES), jnp.float32)

    def make(t):
        p = chip_to(t)
        qs = pl.ds(pl.multiple_of(p * 384, 128), 384)
        ks = pl.ds(pl.multiple_of(p * 256, 128), 256)
        qv = (
            MOMENTUM_DECAY * qm_ref[:, qs].astype(jnp.float32) + qg_ref[:, qs].astype(jnp.float32)
        ).astype(jnp.bfloat16)
        kv = (
            MOMENTUM_DECAY * km_ref[:, ks].astype(jnp.float32) + kg_ref[:, ks].astype(jnp.float32)
        ).astype(jnp.bfloat16)
        qv_ref[:, qs] = qv
        kv_ref[:, ks] = kv
        qv = qv.astype(jnp.float32)
        kv = kv.astype(jnp.float32)
        middle = qv[:, 128:256]
        turned = half_roll(middle)
        low = jnp.concatenate([middle[16:24], zero8], axis=0)
        low_turned = jnp.concatenate([turned[16:24], zero8], axis=0)
        even = 2 * t + core
        odd = 2 * t + 1 - core
        send[even, 0:32, :] = jnp.concatenate([qv[:, 0:128], kv[:, 0:128]], axis=0).astype(
            jnp.bfloat16
        )
        send[even, 32:48, :] = jnp.where(lane16, middle[0:16], low_turned).astype(jnp.bfloat16)
        send[odd, 0:32, :] = jnp.concatenate([qv[:, 256:384], kv[:, 128:256]], axis=0).astype(
            jnp.bfloat16
        )
        send[odd, 32:48, :] = jnp.where(lane16, turned[0:16], low).astype(jnp.bfloat16)

    def out_copy(t, dc):
        j = 2 * t + dc
        return pltpu.make_async_remote_copy(
            src_ref=send.at[j],
            dst_ref=recv.at[j],
            send_sem=send_sem,
            recv_sem=recv_sem.at[lax.div(j, group)],
            device_id=(me_c, 2 * chip_to(t) + core_at(dc)),
            device_id_type=MESH,
        )

    def back_copy(t, dc):
        j = 2 * t + dc
        return pltpu.make_async_remote_copy(
            src_ref=back.at[j],
            dst_ref=home.at[j],
            send_sem=back_sem,
            recv_sem=home_sem.at[lax.div(j, group)],
            device_id=(me_c, 2 * chip_from(t) + core_at(dc)),
            device_id_type=MESH,
        )

    def span(buffer_out, buffer_in, first, size, out_sem, in_sem):
        return pltpu.make_async_remote_copy(
            src_ref=buffer_out.at[pl.ds(first, size)],
            dst_ref=buffer_in.at[pl.ds(first, size)],
            send_sem=out_sem,
            recv_sem=in_sem,
            device_id=(me_c, me),
            device_id_type=MESH,
        )

    opposite = [(dx, dc) for dx in range(nx) for dc in range(2)]

    def aside(dx, dc):
        step = quarter if (dx + dc) % 2 == 0 else nz - quarter
        return lax.rem(z0 + step, nz)

    def first_leg(source, target, out_sem, in_sem, sign):
        for dx, dc in opposite:
            j = 2 * (direct + dx) + dc
            x = lax.rem(x0 + nx + sign * dx, nx)
            pltpu.make_async_remote_copy(
                src_ref=source.at[j],
                dst_ref=target.at[2 * dx + dc],
                send_sem=out_sem,
                recv_sem=in_sem,
                device_id=(me_c, 2 * (x * nz + aside(dx, dc)) + core_at(dc)),
                device_id_type=MESH,
            ).start()

    def second_leg(source, target, out_sem, in_sem):
        for dx, dc in opposite:
            j = 2 * (direct + dx) + dc
            pltpu.make_async_remote_copy(
                src_ref=source.at[2 * dx + dc],
                dst_ref=target.at[j],
                send_sem=out_sem,
                recv_sem=in_sem,
                device_id=(me_c, 2 * (x0 * nz + aside(dx, dc)) + core),
                device_id_type=MESH,
            ).start()

    make(0)
    recv[0] = send[0]
    for dx in range(nx):
        make(direct + dx)
    pl.semaphore_wait(barrier, owners - 1 + n_ctx - 1)
    first_leg(send, relay, send_sem, relay_sem.at[0], 1)
    out_copy(0, 1).start()

    def send_some(first, last):
        @pl.loop(first, last)
        def _(t):
            make(t)
            out_copy(t, 0).start()
            out_copy(t, 1).start()

    send_some(1, direct // 2)
    span(relay, relay, 0, group, send_sem, relay_sem.at[0]).wait_recv()
    second_leg(relay, recv, relay_sem.at[1], recv_sem.at[groups - 1])
    send_some(direct // 2, direct)

    @pl.loop(1, n_ctx)
    def _(i):
        other = lax.rem(me_c + i, n_ctx)
        pltpu.make_async_remote_copy(
            src_ref=lsend.at[other],
            dst_ref=lrecv.at[i],
            send_sem=lsend_sem,
            recv_sem=lrecv_sem,
            device_id=(other, me),
            device_id_type=MESH,
        ).start()

    rows = group * 32
    row = lax.rem(lax.broadcasted_iota(jnp.int32, (rows, LANES), 0), 32)
    is_query = row < 24
    lane = lax.broadcasted_iota(jnp.int32, (group * 16, LANES), 1) < ROPE

    def gather(k):
        first = pl.multiple_of(k * rows, rows)
        block = recv[pl.ds(k * group, group), 0:32, :].reshape(rows, LANES).astype(jnp.float32)
        third = recv[pl.ds(k * group, group), 32:48, :].reshape(group * 16, LANES)
        third = third.astype(jnp.float32)
        top = jnp.where(lane, third, 0.0).reshape(group, 16, LANES)
        bottom = jnp.where(lane, half_roll(third), 0.0).reshape(group, 16, LANES)
        third = jnp.concatenate([top, bottom], axis=1).reshape(rows, LANES)
        query = jnp.where(is_query, block, 0.0).astype(jnp.bfloat16)
        key = jnp.where(is_query, 0.0, block).astype(jnp.bfloat16)
        full = jnp.concatenate([query, third.astype(jnp.bfloat16)], axis=1)
        wide[pl.ds(first, rows), 0:256] = full
        wide[pl.ds(first, rows), 256:384] = key
        gram_q[...] += gram_of(full)
        gram_k[...] += gram_of(key)

    gram_q[...] = jnp.zeros_like(gram_q)
    gram_k[...] = jnp.zeros_like(gram_k)
    span(send, recv, 1, group - 1, send_sem, recv_sem.at[0]).wait_recv()
    gather(0)

    @pl.loop(1, groups)
    def _(k):
        span(send, recv, k * group, group, send_sem, recv_sem.at[k]).wait_recv()
        gather(k)

    mq, mk = newton([begin(gram_q[...], WIDTH), begin(gram_k[...], NOPE)])
    mq_high, mq_low = split(square(mq))
    mk_high, mk_low = split(mk)

    def give(k):
        first = pl.multiple_of(k * rows, rows)
        query = low_dot(wide[pl.ds(first, rows), 0:256], mq_high, mq_low)
        key = low_dot(wide[pl.ds(first, rows), 256:384], mk_high, mk_low)
        block = query[:, 0:128] + key
        third = query[:, 128:256].reshape(group, 32, LANES)
        top = third[:, 0:16].reshape(group * 16, LANES)
        bottom = half_roll(third[:, 16:32].reshape(group * 16, LANES))
        third = jnp.where(lane, top, bottom)
        back[pl.ds(k * group, group), 0:32, :] = block.astype(jnp.bfloat16).reshape(
            group, 32, LANES
        )
        back[pl.ds(k * group, group), 32:48, :] = third.astype(jnp.bfloat16).reshape(
            group, 16, LANES
        )

    give(groups - 1)
    first_leg(back, relay_back, back_sem, relay_sem.at[2], -1)
    give(0)
    back_copy(0, 1).start()
    for t in range(1, pairs):
        back_copy(t, 0).start()
        back_copy(t, 1).start()
    home[0] = back[0]

    def give_some(first, last):
        @pl.loop(first, last)
        def _(k):
            give(k)

            @pl.loop(0, pairs)
            def _(i):
                back_copy(k * pairs + i, 0).start()
                back_copy(k * pairs + i, 1).start()

    give_some(1, groups // 2)
    span(relay_back, relay_back, 0, group, back_sem, relay_sem.at[2]).wait_recv()
    second_leg(relay_back, home, relay_sem.at[3], home_sem.at[groups - 1])
    give_some(groups // 2, groups - 1)

    lrecv[0] = lsend[me_c]
    pltpu.make_async_remote_copy(
        src_ref=lsend.at[pl.ds(1, n_ctx - 1)],
        dst_ref=lrecv.at[pl.ds(1, n_ctx - 1)],
        send_sem=lsend_sem,
        recv_sem=lrecv_sem,
        device_id=(me_c, me),
        device_id_type=MESH,
    ).wait()
    rowmax = jnp.max(lrecv[...], axis=0)[0:1, 0:heads]
    loads[5].wait()
    order = order_ref[pl.ds(me_c, 1), :]
    hit = jnp.broadcast_to(order, (heads, heads)) == lax.broadcasted_iota(
        jnp.int32, (heads, heads), 0
    )
    logit_max = jnp.sum(
        jnp.where(hit, jnp.broadcast_to(rowmax, (heads, heads)), 0.0), axis=1, keepdims=True
    )
    clip = jnp.minimum(1.0, CLIP_LIMIT / logit_max)
    gamma[...] = jnp.broadcast_to(clip, (heads, LANES))
    root[...] = jnp.broadcast_to(jnp.sqrt(clip), (heads, LANES))

    for load in loads[6:]:
        load.wait()
    keep = 1.0 - LEARN_RATE * WEIGHT_DECAY
    rate_q = LEARN_RATE * (0.2 * math.sqrt(max(QR, WIDTH)))
    rate_k = LEARN_RATE * (0.2 * math.sqrt(max(KR, NOPE)))
    lane1 = lax.broadcasted_iota(jnp.int32, (1, LANES), 1) < ROPE

    def finish(t):
        p = chip_to(t)
        even = home[2 * t + core].astype(jnp.float32)
        odd = home[2 * t + 1 - core].astype(jnp.float32)
        even_third, odd_third = even[32:48], odd[32:48]
        even_turned, odd_turned = half_roll(even_third), half_roll(odd_third)
        middle = jnp.concatenate(
            [
                jnp.where(lane16, even_third, odd_turned),
                jnp.where(lane16, even_turned, odd_third)[0:8],
            ],
            axis=0,
        )
        g_even, g_odd = gamma[pl.ds(2 * p, 1), :], gamma[pl.ds(2 * p + 1, 1), :]
        r_even, r_odd = root[pl.ds(2 * p, 1), :], root[pl.ds(2 * p + 1, 1), :]
        tiles = (
            (even[0:24], r_even),
            (middle, jnp.where(lane1, g_even, r_odd)),
            (odd[0:24], jnp.where(lane1, r_odd, g_odd)),
        )
        done = []
        for i, (ortho, factor) in enumerate(tiles):
            at = pl.ds(pl.multiple_of(p * 384 + i * 128, 128), 128)
            done.append((qf_ref, at, (qw_ref[:, at] * keep - rate_q * ortho) * factor))
        for i, (ortho, factor) in enumerate(((even[24:32], r_even), (odd[24:32], r_odd))):
            at = pl.ds(pl.multiple_of(p * 256 + i * 128, 128), 128)
            done.append((kf_ref, at, (kw_ref[:, at] * keep - rate_k * ortho) * factor))
        return done

    def finish_group(k):
        done = []
        for i in range(pairs):
            done += finish(k * pairs + i)
        for ref, at, value in done:
            ref[:, at] = value

    span(back, home, 1, group - 1, back_sem, home_sem.at[0]).wait_recv()
    finish_group(0)

    @pl.loop(1, groups - 1)
    def _(k):
        span(back, home, k * group, group, back_sem, home_sem.at[k]).wait_recv()
        finish_group(k)

    last = (groups - 1) * group
    span(back, home, last, group, back_sem, home_sem.at[groups - 1]).wait_recv()
    finish_group(groups - 1)

    span(relay, relay, 0, group, relay_sem.at[1], relay_sem.at[0]).wait_send()
    span(relay_back, relay_back, 0, group, relay_sem.at[3], relay_sem.at[2]).wait_send()
    span(send, recv, 1, owners - 1, send_sem, recv_sem.at[0]).wait_send()
    span(back, home, 1, owners - 1, back_sem, home_sem.at[0]).wait_send()


def emit(*refs):
    sem = refs[8]
    copies = [pltpu.make_async_copy(refs[i], refs[4 + i], sem.at[i]) for i in range(4)]
    for copy in copies:
        copy.start()
    for copy in copies:
        copy.wait()


def local(
    logit_partial,
    head_order,
    query_weight,
    query_moment,
    query_grad,
    key_weight,
    key_moment,
    key_grad,
):
    owners = lax.axis_size("zero")
    n_ctx = lax.axis_size("ctx")
    group = 8 if owners == 64 else 2
    groups = owners // group
    heads = head_order.shape[1]
    query, key = query_weight.shape[1:], key_weight.shape[1:]
    vmem = pl.BlockSpec(memory_space=pltpu.VMEM)
    hbm = pl.BlockSpec(memory_space=pltpu.HBM)
    dma = pltpu.SemaphoreType.DMA
    shapes = (
        jax.ShapeDtypeStruct(query, jnp.float32),
        jax.ShapeDtypeStruct(query, jnp.bfloat16),
        jax.ShapeDtypeStruct(key, jnp.float32),
        jax.ShapeDtypeStruct(key, jnp.bfloat16),
    )
    results = pl.pallas_call(
        functools.partial(body, owners, n_ctx),
        out_shape=shapes,
        in_specs=[hbm] * 8,
        out_specs=(vmem, vmem, vmem, vmem),
        scratch_shapes=[
            pltpu.VMEM((owners, ROWS, LANES), jnp.bfloat16),
            pltpu.VMEM((owners, ROWS, LANES), jnp.bfloat16),
            pltpu.VMEM((owners, ROWS, LANES), jnp.bfloat16),
            pltpu.VMEM((owners, ROWS, LANES), jnp.bfloat16),
            pltpu.VMEM((group, ROWS, LANES), jnp.bfloat16),
            pltpu.VMEM((group, ROWS, LANES), jnp.bfloat16),
            pltpu.VMEM((owners * 32, 384), jnp.bfloat16),
            pltpu.VMEM((256, 256), jnp.float32),
            pltpu.VMEM((128, 128), jnp.float32),
            pltpu.VMEM((n_ctx, 8, LANES), jnp.float32),
            pltpu.VMEM((n_ctx, 8, LANES), jnp.float32),
            pltpu.VMEM((heads, LANES), jnp.float32),
            pltpu.VMEM((heads, LANES), jnp.float32),
            pltpu.VMEM(query, jnp.float32),
            pltpu.VMEM(key, jnp.float32),
            pltpu.VMEM(query, jnp.bfloat16),
            pltpu.VMEM(query, jnp.bfloat16),
            pltpu.VMEM(key, jnp.bfloat16),
            pltpu.VMEM(key, jnp.bfloat16),
            pltpu.VMEM(logit_partial.shape[1:], jnp.float32),
            pltpu.VMEM(head_order.shape, jnp.int32),
            dma,
            dma((groups,)),
            dma,
            dma((groups,)),
            dma((4,)),
            dma,
            dma,
            dma((8,)),
        ],
        compiler_params=pltpu.CompilerParams(
            collective_id=0, has_side_effects=True, vmem_limit_bytes=48 * 1024 * 1024
        ),
        name="muon",
    )(
        *(
            pltpu.with_memory_space_constraint(array, pltpu.HBM)
            for array in (
                logit_partial[0],
                head_order,
                query_weight[0],
                query_moment[0],
                query_grad[0],
                key_weight[0],
                key_moment[0],
                key_grad[0],
            )
        )
    )
    results = pl.pallas_call(
        emit,
        out_shape=shapes,
        in_specs=[vmem] * 4,
        out_specs=[hbm] * 4,
        scratch_shapes=[dma((4,))],
        compiler_params=pltpu.CompilerParams(vmem_limit_bytes=8 * 1024 * 1024),
        name="emit",
    )(*(pltpu.with_memory_space_constraint(result, pltpu.VMEM) for result in results))
    return tuple(result[None] for result in results)


def solution(mesh):
    shard = P("ctx", "zero", None)
    return jax.shard_map(
        local,
        mesh=mesh,
        in_specs=(P("ctx", None, None), P(), shard, shard, shard, shard, shard, shard),
        out_specs=(shard, shard, shard, shard),
        check_vma=False,
    )
```

```python
import functools
import math

import jax
import jax.numpy as jnp
from jax import lax
from jax.experimental import pallas as pl
from jax.experimental.pallas import tpu as pltpu
from jax.sharding import PartitionSpec as P

QR = 1536
KR = 512
NOPE = 128
ROPE = 64
WIDTH = NOPE + ROPE
ITERS = 5
LANES = 128
ROWS = 48


MOMENTUM_DECAY = 0.95
LEARN_RATE = 0.02
WEIGHT_DECAY = 0.1
CLIP_LIMIT = 100.0
NEWTON_FIRST = 3.4445
NEWTON_SECOND = -4.775
NEWTON_THIRD = 2.0315
NORM_EPSILON = 1e-07
HIGHEST = lax.Precision.HIGHEST
MESH = pl.DeviceIdType.MESH


def gram_of(x):
    return lax.dot_general(x, x, (((0,), (0,)), ((), ())), preferred_element_type=jnp.float32)


def mul(a, b):
    return lax.dot_general(
        a, b, (((1,), (0,)), ((), ())), precision=HIGHEST, preferred_element_type=jnp.float32
    )


def low_dot(x, high, low):
    return jnp.dot(x, high, preferred_element_type=jnp.float32) + jnp.dot(
        x, low, preferred_element_type=jnp.float32
    )


def begin(gram, size):
    gram = gram[0:size]
    eye = lax.broadcasted_iota(jnp.int32, gram.shape, 0) == lax.broadcasted_iota(
        jnp.int32, gram.shape, 1
    )
    total = jnp.sum(jnp.where(eye, gram, 0.0), axis=1, keepdims=True)
    total = jnp.sum(total, axis=0, keepdims=True)
    inverse = 1.0 / (jnp.sqrt(total) + NORM_EPSILON)
    return gram * inverse * inverse, inverse, jnp.where(eye, 1.0, 0.0)


def square(x):
    missing = x.shape[1] - x.shape[0]
    if not missing:
        return x
    return jnp.concatenate([x, jnp.zeros((missing, x.shape[1]), x.dtype)], axis=0)


def split(m):
    high = m.astype(jnp.bfloat16)
    return high, (m - high.astype(jnp.float32)).astype(jnp.bfloat16)


def mul3(a, b):
    b_high, b_low = square(b[0]), square(b[1])
    return (
        jnp.dot(a[0], b_high, preferred_element_type=jnp.float32)
        + jnp.dot(a[0], b_low, preferred_element_type=jnp.float32)
        + jnp.dot(a[1], b_high, preferred_element_type=jnp.float32)
    )


def stack(a, b):
    return tuple(jnp.concatenate(pair, axis=0) for pair in zip(a, b))


def newton(grams):
    a, inverse, eye = (list(x) for x in zip(*grams))
    m = [None] * len(a)
    which = range(len(a))
    for sweep in range(ITERS):
        exact = sweep == 0
        halves = [split(a[i]) for i in which]
        if exact:
            s = [mul(a[i], square(a[i])) for i in which]
        else:
            s = [mul3(halves[i], halves[i]) for i in which]
        p = [NEWTON_FIRST * eye[i] + NEWTON_SECOND * a[i] + NEWTON_THIRD * s[i] for i in which]
        p_halves = [split(p[i]) for i in which]
        if exact:
            y = [mul(a[i], square(p[i])) for i in which]
            a = [mul(y[i], square(p[i])) for i in which]
            m = p
        elif sweep < ITERS - 1:
            both = [mul3(stack(halves[i], split(m[i])), p_halves[i]) for i in which]
            size = [a[i].shape[0] for i in which]
            a = [mul3(split(both[i][0 : size[i]]), p_halves[i]) for i in which]
            m = [both[i][size[i] :] for i in which]
        else:
            m = [mul3(split(m[i]), p_halves[i]) for i in which]
    return [m[i] * inverse[i] for i in which]


def half_roll(x):
    return pltpu.roll(x, ROPE, 1)


def body(
    owners,
    n_ctx,
    lp_hbm,
    order_hbm,
    qw_hbm,
    qm_hbm,
    qg_hbm,
    kw_hbm,
    km_hbm,
    kg_hbm,
    qf_ref,
    qv_ref,
    kf_ref,
    kv_ref,
    send,
    recv,
    back,
    home,
    wide,
    gram_q,
    gram_k,
    lsend,
    lrecv,
    gamma,
    root,
    qw_ref,
    kw_ref,
    qm_ref,
    qg_ref,
    km_ref,
    kg_ref,
    lp_ref,
    order_ref,
    send_sem,
    recv_sem,
    back_sem,
    home_sem,
    lsend_sem,
    lrecv_sem,
    load_sem,
):
    nx = 4 if owners == 64 else 1
    chips = owners // 2
    nz = chips // nx
    group = 2 * nx
    groups = owners // group
    pairs = group // 2
    me_c = lax.axis_index("ctx")
    me = lax.axis_index("zero")
    core = lax.rem(me, 2)
    chip = lax.div(me, 2)
    x0, z0 = lax.div(chip, nz), lax.rem(chip, nz)

    def core_at(dc):
        return lax.rem(core + dc, 2)

    def offset(t):
        i = lax.rem(t, nz)
        dz = lax.div(i + 1, 2) * (1 - 2 * lax.rem(i + 1, 2))
        dx = lax.rem(i + lax.div(t, nz), nx)
        return dx, dz

    def chip_to(t):
        dx, dz = offset(t)
        way = 1 - 2 * core
        return lax.rem(x0 + way * dx + nx, nx) * nz + lax.rem(z0 + way * dz + nz, nz)

    def chip_from(t, dc):
        dx, dz = offset(t)
        way = 1 - 2 * core_at(dc)
        return lax.rem(x0 - way * dx + nx, nx) * nz + lax.rem(z0 - way * dz + nz, nz)

    loads = [
        pltpu.make_async_copy(source, target, load_sem.at[i])
        for i, (source, target) in enumerate(
            (
                (qm_hbm, qm_ref),
                (qg_hbm, qg_ref),
                (km_hbm, km_ref),
                (kg_hbm, kg_ref),
                (lp_hbm, lp_ref),
                (order_hbm, order_ref),
                (qw_hbm, qw_ref),
                (kw_hbm, kw_ref),
            )
        )
    ]
    for load in loads:
        load.start()

    barrier = pltpu.get_barrier_semaphore()

    @pl.loop(1, owners)
    def _(i):
        pl.semaphore_signal(
            barrier, inc=1, device_id=(me_c, lax.rem(me + i, owners)), device_id_type=MESH
        )

    @pl.loop(1, n_ctx)
    def _(i):
        pl.semaphore_signal(
            barrier, inc=1, device_id=(lax.rem(me_c + i, n_ctx), me), device_id_type=MESH
        )

    heads = lp_ref.shape[1]
    for load in loads[:5]:
        load.wait()
    for layer in range(n_ctx):
        lsend[layer, :, 0:heads] = jnp.broadcast_to(lp_ref[layer : layer + 1, :], (8, heads))
        lsend[layer, :, heads:] = jnp.zeros((8, LANES - heads), jnp.float32)

    lane16 = lax.broadcasted_iota(jnp.int32, (16, LANES), 1) < ROPE
    zero8 = jnp.zeros((8, LANES), jnp.float32)

    def make(t):
        p = chip_to(t)
        qs = pl.ds(pl.multiple_of(p * 384, 128), 384)
        ks = pl.ds(pl.multiple_of(p * 256, 128), 256)
        qv = (
            MOMENTUM_DECAY * qm_ref[:, qs].astype(jnp.float32) + qg_ref[:, qs].astype(jnp.float32)
        ).astype(jnp.bfloat16)
        kv = (
            MOMENTUM_DECAY * km_ref[:, ks].astype(jnp.float32) + kg_ref[:, ks].astype(jnp.float32)
        ).astype(jnp.bfloat16)
        qv_ref[:, qs] = qv
        kv_ref[:, ks] = kv
        qv = qv.astype(jnp.float32)
        kv = kv.astype(jnp.float32)
        middle = qv[:, 128:256]
        turned = half_roll(middle)
        low = jnp.concatenate([middle[16:24], zero8], axis=0)
        low_turned = jnp.concatenate([turned[16:24], zero8], axis=0)
        even = 2 * t + core
        odd = 2 * t + 1 - core
        send[even, 0:32, :] = jnp.concatenate([qv[:, 0:128], kv[:, 0:128]], axis=0).astype(
            jnp.bfloat16
        )
        send[even, 32:48, :] = jnp.where(lane16, middle[0:16], low_turned).astype(jnp.bfloat16)
        send[odd, 0:32, :] = jnp.concatenate([qv[:, 256:384], kv[:, 128:256]], axis=0).astype(
            jnp.bfloat16
        )
        send[odd, 32:48, :] = jnp.where(lane16, turned[0:16], low).astype(jnp.bfloat16)

    def out_copy(t, dc):
        j = 2 * t + dc
        return pltpu.make_async_remote_copy(
            src_ref=send.at[j],
            dst_ref=recv.at[j],
            send_sem=send_sem,
            recv_sem=recv_sem.at[lax.div(j, group)],
            device_id=(me_c, 2 * chip_to(t) + core_at(dc)),
            device_id_type=MESH,
        )

    def back_copy(t, dc):
        j = 2 * t + dc
        return pltpu.make_async_remote_copy(
            src_ref=back.at[j],
            dst_ref=home.at[j],
            send_sem=back_sem,
            recv_sem=home_sem.at[lax.div(j, group)],
            device_id=(me_c, 2 * chip_from(t, dc) + core_at(dc)),
            device_id_type=MESH,
        )

    def span(buffer_out, buffer_in, first, size, out_sem, in_sem):
        return pltpu.make_async_remote_copy(
            src_ref=buffer_out.at[pl.ds(first, size)],
            dst_ref=buffer_in.at[pl.ds(first, size)],
            send_sem=out_sem,
            recv_sem=in_sem,
            device_id=(me_c, me),
            device_id_type=MESH,
        )

    make(0)
    recv[0] = send[0]
    pl.semaphore_wait(barrier, owners - 1 + n_ctx - 1)
    out_copy(0, 1).start()

    @pl.loop(1, chips)
    def _(t):
        make(t)
        out_copy(t, 0).start()
        out_copy(t, 1).start()

    @pl.loop(1, n_ctx)
    def _(i):
        other = lax.rem(me_c + i, n_ctx)
        pltpu.make_async_remote_copy(
            src_ref=lsend.at[other],
            dst_ref=lrecv.at[i],
            send_sem=lsend_sem,
            recv_sem=lrecv_sem,
            device_id=(other, me),
            device_id_type=MESH,
        ).start()

    rows = group * 32
    row = lax.rem(lax.broadcasted_iota(jnp.int32, (rows, LANES), 0), 32)
    is_query = row < 24
    lane = lax.broadcasted_iota(jnp.int32, (group * 16, LANES), 1) < ROPE

    def gather(k):
        first = pl.multiple_of(k * rows, rows)
        block = recv[pl.ds(k * group, group), 0:32, :].reshape(rows, LANES).astype(jnp.float32)
        third = recv[pl.ds(k * group, group), 32:48, :].reshape(group * 16, LANES)
        third = third.astype(jnp.float32)
        top = jnp.where(lane, third, 0.0).reshape(group, 16, LANES)
        bottom = jnp.where(lane, half_roll(third), 0.0).reshape(group, 16, LANES)
        third = jnp.concatenate([top, bottom], axis=1).reshape(rows, LANES)
        query = jnp.where(is_query, block, 0.0).astype(jnp.bfloat16)
        key = jnp.where(is_query, 0.0, block).astype(jnp.bfloat16)
        full = jnp.concatenate([query, third.astype(jnp.bfloat16)], axis=1)
        wide[pl.ds(first, rows), 0:256] = full
        wide[pl.ds(first, rows), 256:384] = key
        gram_q[...] += gram_of(full)
        gram_k[...] += gram_of(key)

    gram_q[...] = jnp.zeros_like(gram_q)
    gram_k[...] = jnp.zeros_like(gram_k)
    span(send, recv, 1, group - 1, send_sem, recv_sem.at[0]).wait_recv()
    gather(0)

    @pl.loop(1, groups)
    def _(k):
        span(send, recv, k * group, group, send_sem, recv_sem.at[k]).wait_recv()
        gather(k)

    mq, mk = newton([begin(gram_q[...], WIDTH), begin(gram_k[...], NOPE)])
    mq_high, mq_low = split(square(mq))
    mk_high, mk_low = split(mk)

    def give(k):
        first = pl.multiple_of(k * rows, rows)
        query = low_dot(wide[pl.ds(first, rows), 0:256], mq_high, mq_low)
        key = low_dot(wide[pl.ds(first, rows), 256:384], mk_high, mk_low)
        block = query[:, 0:128] + key
        third = query[:, 128:256].reshape(group, 32, LANES)
        top = third[:, 0:16].reshape(group * 16, LANES)
        bottom = half_roll(third[:, 16:32].reshape(group * 16, LANES))
        third = jnp.where(lane, top, bottom)
        back[pl.ds(k * group, group), 0:32, :] = block.astype(jnp.bfloat16).reshape(
            group, 32, LANES
        )
        back[pl.ds(k * group, group), 32:48, :] = third.astype(jnp.bfloat16).reshape(
            group, 16, LANES
        )

    give(0)
    back_copy(0, 1).start()
    for t in range(1, pairs):
        back_copy(t, 0).start()
        back_copy(t, 1).start()
    home[0] = back[0]

    @pl.loop(1, groups)
    def _(k):
        give(k)

        @pl.loop(0, pairs)
        def _(i):
            back_copy(k * pairs + i, 0).start()
            back_copy(k * pairs + i, 1).start()

    lrecv[0] = lsend[me_c]
    pltpu.make_async_remote_copy(
        src_ref=lsend.at[pl.ds(1, n_ctx - 1)],
        dst_ref=lrecv.at[pl.ds(1, n_ctx - 1)],
        send_sem=lsend_sem,
        recv_sem=lrecv_sem,
        device_id=(me_c, me),
        device_id_type=MESH,
    ).wait()
    rowmax = jnp.max(lrecv[...], axis=0)[0:1, 0:heads]
    loads[5].wait()
    order = order_ref[pl.ds(me_c, 1), :]
    hit = jnp.broadcast_to(order, (heads, heads)) == lax.broadcasted_iota(
        jnp.int32, (heads, heads), 0
    )
    logit_max = jnp.sum(
        jnp.where(hit, jnp.broadcast_to(rowmax, (heads, heads)), 0.0), axis=1, keepdims=True
    )
    clip = jnp.minimum(1.0, CLIP_LIMIT / logit_max)
    gamma[...] = jnp.broadcast_to(clip, (heads, LANES))
    root[...] = jnp.broadcast_to(jnp.sqrt(clip), (heads, LANES))

    for load in loads[6:]:
        load.wait()
    keep = 1.0 - LEARN_RATE * WEIGHT_DECAY
    rate_q = LEARN_RATE * (0.2 * math.sqrt(max(QR, WIDTH)))
    rate_k = LEARN_RATE * (0.2 * math.sqrt(max(KR, NOPE)))
    lane1 = lax.broadcasted_iota(jnp.int32, (1, LANES), 1) < ROPE

    def finish(t):
        p = chip_to(t)
        even = home[2 * t + core].astype(jnp.float32)
        odd = home[2 * t + 1 - core].astype(jnp.float32)
        even_third, odd_third = even[32:48], odd[32:48]
        even_turned, odd_turned = half_roll(even_third), half_roll(odd_third)
        middle = jnp.concatenate(
            [
                jnp.where(lane16, even_third, odd_turned),
                jnp.where(lane16, even_turned, odd_third)[0:8],
            ],
            axis=0,
        )
        g_even, g_odd = gamma[pl.ds(2 * p, 1), :], gamma[pl.ds(2 * p + 1, 1), :]
        r_even, r_odd = root[pl.ds(2 * p, 1), :], root[pl.ds(2 * p + 1, 1), :]
        tiles = (
            (even[0:24], r_even),
            (middle, jnp.where(lane1, g_even, r_odd)),
            (odd[0:24], jnp.where(lane1, r_odd, g_odd)),
        )
        done = []
        for i, (ortho, factor) in enumerate(tiles):
            at = pl.ds(pl.multiple_of(p * 384 + i * 128, 128), 128)
            done.append((qf_ref, at, (qw_ref[:, at] * keep - rate_q * ortho) * factor))
        for i, (ortho, factor) in enumerate(((even[24:32], r_even), (odd[24:32], r_odd))):
            at = pl.ds(pl.multiple_of(p * 256 + i * 128, 128), 128)
            done.append((kf_ref, at, (kw_ref[:, at] * keep - rate_k * ortho) * factor))
        return done

    def finish_group(k):
        done = []
        for i in range(pairs):
            done += finish(k * pairs + i)
        for ref, at, value in done:
            ref[:, at] = value

    span(back, home, 1, group - 1, back_sem, home_sem.at[0]).wait_recv()
    finish_group(0)

    @pl.loop(1, groups)
    def _(k):
        span(back, home, k * group, group, back_sem, home_sem.at[k]).wait_recv()
        finish_group(k)

    span(send, recv, 1, owners - 1, send_sem, recv_sem.at[0]).wait_send()
    span(back, home, 1, owners - 1, back_sem, home_sem.at[0]).wait_send()


def emit(*refs):
    sem = refs[8]
    copies = [pltpu.make_async_copy(refs[i], refs[4 + i], sem.at[i]) for i in range(4)]
    for copy in copies:
        copy.start()
    for copy in copies:
        copy.wait()


def local(
    logit_partial,
    head_order,
    query_weight,
    query_moment,
    query_grad,
    key_weight,
    key_moment,
    key_grad,
):
    owners = lax.axis_size("zero")
    n_ctx = lax.axis_size("ctx")
    group = 8 if owners == 64 else 2
    groups = owners // group
    heads = head_order.shape[1]
    query, key = query_weight.shape[1:], key_weight.shape[1:]
    vmem = pl.BlockSpec(memory_space=pltpu.VMEM)
    hbm = pl.BlockSpec(memory_space=pltpu.HBM)
    dma = pltpu.SemaphoreType.DMA
    shapes = (
        jax.ShapeDtypeStruct(query, jnp.float32),
        jax.ShapeDtypeStruct(query, jnp.bfloat16),
        jax.ShapeDtypeStruct(key, jnp.float32),
        jax.ShapeDtypeStruct(key, jnp.bfloat16),
    )
    results = pl.pallas_call(
        functools.partial(body, owners, n_ctx),
        out_shape=shapes,
        in_specs=[hbm] * 8,
        out_specs=(vmem, vmem, vmem, vmem),
        scratch_shapes=[
            pltpu.VMEM((owners, ROWS, LANES), jnp.bfloat16),
            pltpu.VMEM((owners, ROWS, LANES), jnp.bfloat16),
            pltpu.VMEM((owners, ROWS, LANES), jnp.bfloat16),
            pltpu.VMEM((owners, ROWS, LANES), jnp.bfloat16),
            pltpu.VMEM((owners * 32, 384), jnp.bfloat16),
            pltpu.VMEM((256, 256), jnp.float32),
            pltpu.VMEM((128, 128), jnp.float32),
            pltpu.VMEM((n_ctx, 8, LANES), jnp.float32),
            pltpu.VMEM((n_ctx, 8, LANES), jnp.float32),
            pltpu.VMEM((heads, LANES), jnp.float32),
            pltpu.VMEM((heads, LANES), jnp.float32),
            pltpu.VMEM(query, jnp.float32),
            pltpu.VMEM(key, jnp.float32),
            pltpu.VMEM(query, jnp.bfloat16),
            pltpu.VMEM(query, jnp.bfloat16),
            pltpu.VMEM(key, jnp.bfloat16),
            pltpu.VMEM(key, jnp.bfloat16),
            pltpu.VMEM(logit_partial.shape[1:], jnp.float32),
            pltpu.VMEM(head_order.shape, jnp.int32),
            dma,
            dma((groups,)),
            dma,
            dma((groups,)),
            dma,
            dma,
            dma((8,)),
        ],
        compiler_params=pltpu.CompilerParams(
            collective_id=0, has_side_effects=True, vmem_limit_bytes=48 * 1024 * 1024
        ),
        name="muon",
    )(
        *(
            pltpu.with_memory_space_constraint(array, pltpu.HBM)
            for array in (
                logit_partial[0],
                head_order,
                query_weight[0],
                query_moment[0],
                query_grad[0],
                key_weight[0],
                key_moment[0],
                key_grad[0],
            )
        )
    )
    results = pl.pallas_call(
        emit,
        out_shape=shapes,
        in_specs=[vmem] * 4,
        out_specs=[hbm] * 4,
        scratch_shapes=[dma((4,))],
        compiler_params=pltpu.CompilerParams(vmem_limit_bytes=8 * 1024 * 1024),
        name="emit",
    )(*(pltpu.with_memory_space_constraint(result, pltpu.VMEM) for result in results))
    return tuple(result[None] for result in results)


def solution(mesh):
    shard = P("ctx", "zero", None)
    return jax.shard_map(
        local,
        mesh=mesh,
        in_specs=(P("ctx", None, None), P(), shard, shard, shard, shard, shard, shard),
        out_specs=(shard, shard, shard, shard),
        check_vma=False,
    )
```

```python
import functools
import math

import jax
import jax.numpy as jnp
from jax import lax
from jax.experimental import pallas as pl
from jax.experimental.pallas import tpu as pltpu
from jax.sharding import PartitionSpec as P

QR = 1536
KR = 512
NOPE = 128
ROPE = 64
WIDTH = NOPE + ROPE
ITERS = 5
LANES = 128
ROWS = 48


MOMENTUM_DECAY = 0.95
LEARN_RATE = 0.02
WEIGHT_DECAY = 0.1
CLIP_LIMIT = 100.0
NEWTON_FIRST = 3.4445
NEWTON_SECOND = -4.775
NEWTON_THIRD = 2.0315
NORM_EPSILON = 1e-07
HIGHEST = lax.Precision.HIGHEST
MESH = pl.DeviceIdType.MESH


def gram_of(x):
    return lax.dot_general(x, x, (((0,), (0,)), ((), ())), preferred_element_type=jnp.float32)


def begin(gram, size):
    gram = gram[0:size]
    eye = lax.broadcasted_iota(jnp.int32, gram.shape, 0) == lax.broadcasted_iota(
        jnp.int32, gram.shape, 1
    )
    total = jnp.sum(jnp.where(eye, gram, 0.0), axis=1, keepdims=True)
    total = jnp.sum(total, axis=0, keepdims=True)
    inverse = 1.0 / (jnp.sqrt(total) + NORM_EPSILON)
    return gram * inverse * inverse, inverse, jnp.where(eye, 1.0, 0.0)


def square(x):
    missing = x.shape[1] - x.shape[0]
    if not missing:
        return x
    return jnp.concatenate([x, jnp.zeros((missing, x.shape[1]), x.dtype)], axis=0)


def split(m):
    high = m.astype(jnp.bfloat16)
    return high, (m - high.astype(jnp.float32)).astype(jnp.bfloat16)


def split3(m):
    high = m.astype(jnp.bfloat16)
    rest = m - high.astype(jnp.float32)
    middle = rest.astype(jnp.bfloat16)
    return high, middle, (rest - middle.astype(jnp.float32)).astype(jnp.bfloat16)


def joined(lefts, rights):
    return jnp.dot(
        jnp.concatenate(lefts, axis=1),
        jnp.concatenate([square(right) for right in rights], axis=0),
        preferred_element_type=jnp.float32,
    )


def mul3(a, b):
    return joined((a[0], a[0], a[1]), (b[0], b[1], b[0]))


def mul6(a, b):
    return joined((a[0], a[0], a[1], a[1], a[0], a[2]), (b[0], b[1], b[0], b[1], b[2], b[0]))


def stack(a, b):
    return tuple(jnp.concatenate(pair, axis=0) for pair in zip(a, b))


def newton(grams):
    a, inverse, eye = (list(x) for x in zip(*grams))
    m = [None] * len(a)
    which = range(len(a))
    for sweep in range(ITERS):
        exact = sweep == 0
        parts, product = (split3, mul6) if exact else (split, mul3)
        a_parts = [parts(a[i]) for i in which]
        s = [product(a_parts[i], a_parts[i]) for i in which]
        p = [NEWTON_FIRST * eye[i] + NEWTON_SECOND * a[i] + NEWTON_THIRD * s[i] for i in which]
        p_parts = [parts(p[i]) for i in which]
        if exact:
            y = [product(a_parts[i], p_parts[i]) for i in which]
            a = [product(parts(y[i]), p_parts[i]) for i in which]
            m = p
        elif sweep < ITERS - 1:
            both = [product(stack(a_parts[i], parts(m[i])), p_parts[i]) for i in which]
            size = [a[i].shape[0] for i in which]
            a = [product(parts(both[i][0 : size[i]]), p_parts[i]) for i in which]
            m = [both[i][size[i] :] for i in which]
        else:
            m = [product(parts(m[i]), p_parts[i]) for i in which]
    return [m[i] * inverse[i] for i in which]


def half_roll(x):
    return pltpu.roll(x, ROPE, 1)


def body(
    owners,
    n_ctx,
    lp_hbm,
    order_hbm,
    qw_hbm,
    qm_hbm,
    qg_hbm,
    kw_hbm,
    km_hbm,
    kg_hbm,
    qf_ref,
    qv_ref,
    kf_ref,
    kv_ref,
    send,
    recv,
    back,
    home,
    wide,
    factor,
    gram_q,
    gram_k,
    lsend,
    lrecv,
    gamma,
    root,
    qw_ref,
    kw_ref,
    qm_ref,
    qg_ref,
    km_ref,
    kg_ref,
    lp_ref,
    order_ref,
    send_sem,
    recv_sem,
    back_sem,
    home_sem,
    lsend_sem,
    lrecv_sem,
    load_sem,
):
    nx = 4 if owners == 64 else 1
    chips = owners // 2
    nz = chips // nx
    group = 2 * nx
    groups = owners // group
    pairs = group // 2
    me_c = lax.axis_index("ctx")
    me = lax.axis_index("zero")
    core = lax.rem(me, 2)
    chip = lax.div(me, 2)
    x0, z0 = lax.div(chip, nz), lax.rem(chip, nz)

    def core_at(dc):
        return lax.rem(core + dc, 2)

    def offset(t):
        i = lax.rem(t, nz)
        dz = lax.div(i + 1, 2) * (1 - 2 * lax.rem(i + 1, 2))
        dx = lax.rem(i + lax.div(t, nz), nx)
        return dx, dz

    def chip_to(t):
        dx, dz = offset(t)
        way = 1 - 2 * core
        return lax.rem(x0 + way * dx + nx, nx) * nz + lax.rem(z0 + way * dz + nz, nz)

    def chip_from(t, dc):
        dx, dz = offset(t)
        way = 1 - 2 * core_at(dc)
        return lax.rem(x0 - way * dx + nx, nx) * nz + lax.rem(z0 - way * dz + nz, nz)

    loads = [
        pltpu.make_async_copy(source, target, load_sem.at[i])
        for i, (source, target) in enumerate(
            (
                (qm_hbm, qm_ref),
                (qg_hbm, qg_ref),
                (km_hbm, km_ref),
                (kg_hbm, kg_ref),
                (lp_hbm, lp_ref),
                (order_hbm, order_ref),
                (qw_hbm, qw_ref),
                (kw_hbm, kw_ref),
            )
        )
    ]
    for load in loads[:6]:
        load.start()

    barrier = pltpu.get_barrier_semaphore()

    @pl.loop(1, owners)
    def _(i):
        pl.semaphore_signal(
            barrier, inc=1, device_id=(me_c, lax.rem(me + i, owners)), device_id_type=MESH
        )

    @pl.loop(1, n_ctx)
    def _(i):
        pl.semaphore_signal(
            barrier, inc=1, device_id=(lax.rem(me_c + i, n_ctx), me), device_id_type=MESH
        )

    heads = lp_ref.shape[1]
    for load in loads[:4]:
        load.wait()
    for load in loads[6:]:
        load.start()
    lane16 = lax.broadcasted_iota(jnp.int32, (16, LANES), 1) < ROPE
    zero8 = jnp.zeros((8, LANES), jnp.float32)

    def make(t):
        p = chip_to(t)
        qs = pl.ds(pl.multiple_of(p * 384, 128), 384)
        ks = pl.ds(pl.multiple_of(p * 256, 128), 256)
        qv = (
            MOMENTUM_DECAY * qm_ref[:, qs].astype(jnp.float32) + qg_ref[:, qs].astype(jnp.float32)
        ).astype(jnp.bfloat16)
        kv = (
            MOMENTUM_DECAY * km_ref[:, ks].astype(jnp.float32) + kg_ref[:, ks].astype(jnp.float32)
        ).astype(jnp.bfloat16)
        qv_ref[:, qs] = qv
        kv_ref[:, ks] = kv
        qv = qv.astype(jnp.float32)
        kv = kv.astype(jnp.float32)
        middle = qv[:, 128:256]
        turned = half_roll(middle)
        low = jnp.concatenate([middle[16:24], zero8], axis=0)
        low_turned = jnp.concatenate([turned[16:24], zero8], axis=0)
        even = 2 * t + core
        odd = 2 * t + 1 - core
        send[even, 0:32, :] = jnp.concatenate([qv[:, 0:128], kv[:, 0:128]], axis=0).astype(
            jnp.bfloat16
        )
        send[even, 32:48, :] = jnp.where(lane16, middle[0:16], low_turned).astype(jnp.bfloat16)
        send[odd, 0:32, :] = jnp.concatenate([qv[:, 256:384], kv[:, 128:256]], axis=0).astype(
            jnp.bfloat16
        )
        send[odd, 32:48, :] = jnp.where(lane16, turned[0:16], low).astype(jnp.bfloat16)

    def out_copy(t, dc):
        j = 2 * t + dc
        return pltpu.make_async_remote_copy(
            src_ref=send.at[j],
            dst_ref=recv.at[j],
            send_sem=send_sem,
            recv_sem=recv_sem.at[lax.div(j, group)],
            device_id=(me_c, 2 * chip_to(t) + core_at(dc)),
            device_id_type=MESH,
        )

    def back_copy(t, dc):
        j = 2 * t + dc
        return pltpu.make_async_remote_copy(
            src_ref=back.at[j],
            dst_ref=home.at[j],
            send_sem=back_sem,
            recv_sem=home_sem.at[lax.div(j, group)],
            device_id=(me_c, 2 * chip_from(t, dc) + core_at(dc)),
            device_id_type=MESH,
        )

    def span(buffer_out, buffer_in, first, size, out_sem, in_sem):
        return pltpu.make_async_remote_copy(
            src_ref=buffer_out.at[pl.ds(first, size)],
            dst_ref=buffer_in.at[pl.ds(first, size)],
            send_sem=out_sem,
            recv_sem=in_sem,
            device_id=(me_c, me),
            device_id_type=MESH,
        )

    make(0)
    recv[0] = send[0]
    pl.semaphore_wait(barrier, owners - 1 + n_ctx - 1)
    out_copy(0, 1).start()

    @pl.loop(1, chips)
    def _(t):
        make(t)
        out_copy(t, 0).start()
        out_copy(t, 1).start()

    loads[4].wait()
    for layer in range(n_ctx):
        lsend[layer, :, 0:heads] = jnp.broadcast_to(lp_ref[layer : layer + 1, :], (8, heads))
        lsend[layer, :, heads:] = jnp.zeros((8, LANES - heads), jnp.float32)

    @pl.loop(1, n_ctx)
    def _(i):
        other = lax.rem(me_c + i, n_ctx)
        pltpu.make_async_remote_copy(
            src_ref=lsend.at[other],
            dst_ref=lrecv.at[i],
            send_sem=lsend_sem,
            recv_sem=lrecv_sem,
            device_id=(other, me),
            device_id_type=MESH,
        ).start()

    rows = group * 32
    row = lax.rem(lax.broadcasted_iota(jnp.int32, (rows, LANES), 0), 32)
    is_query = row < 24
    lane = lax.broadcasted_iota(jnp.int32, (group * 16, LANES), 1) < ROPE

    def gather(k):
        first = pl.multiple_of(k * rows, rows)
        block = recv[pl.ds(k * group, group), 0:32, :].reshape(rows, LANES).astype(jnp.float32)
        third = recv[pl.ds(k * group, group), 32:48, :].reshape(group * 16, LANES)
        third = third.astype(jnp.float32)
        top = jnp.where(lane, third, 0.0).reshape(group, 16, LANES)
        bottom = jnp.where(lane, half_roll(third), 0.0).reshape(group, 16, LANES)
        third = jnp.concatenate([top, bottom], axis=1).reshape(rows, LANES)
        query = jnp.where(is_query, block, 0.0).astype(jnp.bfloat16)
        key = jnp.where(is_query, 0.0, block).astype(jnp.bfloat16)
        full = jnp.concatenate([query, third.astype(jnp.bfloat16)], axis=1)
        wide[pl.ds(first, rows), 0:256] = full
        wide[pl.ds(first, rows), 256:384] = key
        gram_q[...] += gram_of(full)
        gram_k[...] += gram_of(key)

    gram_q[...] = jnp.zeros_like(gram_q)
    gram_k[...] = jnp.zeros_like(gram_k)
    span(send, recv, 1, group - 1, send_sem, recv_sem.at[0]).wait_recv()
    gather(0)

    @pl.loop(1, groups)
    def _(k):
        span(send, recv, k * group, group, send_sem, recv_sem.at[k]).wait_recv()
        gather(k)

    mq, mk = newton([begin(gram_q[...], WIDTH), begin(gram_k[...], NOPE)])
    mq, mk = split(square(mq)), split(mk)
    for half in range(2):
        first = half * 384
        factor[first : first + 256, :] = mq[half]
        factor[first + 256 : first + 384, 0:128] = mk[half]
        factor[first + 256 : first + 384, 128:256] = jnp.zeros((128, 128), jnp.bfloat16)

    def give(k):
        first = pl.multiple_of(k * rows, rows)
        x = wide[pl.ds(first, rows), :]
        product = jnp.dot(
            jnp.concatenate([x, x], axis=1), factor[...], preferred_element_type=jnp.float32
        )
        block = product[:, 0:128]
        third = product[:, 128:256].reshape(group, 32, LANES)
        top = third[:, 0:16].reshape(group * 16, LANES)
        bottom = half_roll(third[:, 16:32].reshape(group * 16, LANES))
        third = jnp.where(lane, top, bottom)
        back[pl.ds(k * group, group), 0:32, :] = block.astype(jnp.bfloat16).reshape(
            group, 32, LANES
        )
        back[pl.ds(k * group, group), 32:48, :] = third.astype(jnp.bfloat16).reshape(
            group, 16, LANES
        )

    give(0)
    back_copy(0, 1).start()
    for t in range(1, pairs):
        back_copy(t, 0).start()
        back_copy(t, 1).start()
    home[0] = back[0]

    @pl.loop(1, groups)
    def _(k):
        give(k)

        @pl.loop(0, pairs)
        def _(i):
            back_copy(k * pairs + i, 0).start()
            back_copy(k * pairs + i, 1).start()

    lrecv[0] = lsend[me_c]
    pltpu.make_async_remote_copy(
        src_ref=lsend.at[pl.ds(1, n_ctx - 1)],
        dst_ref=lrecv.at[pl.ds(1, n_ctx - 1)],
        send_sem=lsend_sem,
        recv_sem=lrecv_sem,
        device_id=(me_c, me),
        device_id_type=MESH,
    ).wait()
    rowmax = jnp.max(lrecv[...], axis=0)[0:1, 0:heads]
    loads[5].wait()
    order = order_ref[pl.ds(me_c, 1), :]
    hit = jnp.broadcast_to(order, (heads, heads)) == lax.broadcasted_iota(
        jnp.int32, (heads, heads), 0
    )
    logit_max = jnp.sum(
        jnp.where(hit, jnp.broadcast_to(rowmax, (heads, heads)), 0.0), axis=1, keepdims=True
    )
    clip = jnp.minimum(1.0, CLIP_LIMIT / logit_max)
    gamma[...] = jnp.broadcast_to(clip, (heads, LANES))
    root[...] = jnp.broadcast_to(jnp.sqrt(clip), (heads, LANES))

    for load in loads[6:]:
        load.wait()
    keep = 1.0 - LEARN_RATE * WEIGHT_DECAY
    rate_q = LEARN_RATE * (0.2 * math.sqrt(max(QR, WIDTH)))
    rate_k = LEARN_RATE * (0.2 * math.sqrt(max(KR, NOPE)))
    lane1 = lax.broadcasted_iota(jnp.int32, (1, LANES), 1) < ROPE

    def finish(t):
        p = chip_to(t)
        even = home[2 * t + core].astype(jnp.float32)
        odd = home[2 * t + 1 - core].astype(jnp.float32)
        even_third, odd_third = even[32:48], odd[32:48]
        even_turned, odd_turned = half_roll(even_third), half_roll(odd_third)
        middle = jnp.concatenate(
            [
                jnp.where(lane16, even_third, odd_turned),
                jnp.where(lane16, even_turned, odd_third)[0:8],
            ],
            axis=0,
        )
        g_even, g_odd = gamma[pl.ds(2 * p, 1), :], gamma[pl.ds(2 * p + 1, 1), :]
        r_even, r_odd = root[pl.ds(2 * p, 1), :], root[pl.ds(2 * p + 1, 1), :]
        tiles = (
            (even[0:24], r_even),
            (middle, jnp.where(lane1, g_even, r_odd)),
            (odd[0:24], jnp.where(lane1, r_odd, g_odd)),
        )
        done = []
        for i, (ortho, factor) in enumerate(tiles):
            at = pl.ds(pl.multiple_of(p * 384 + i * 128, 128), 128)
            done.append((qf_ref, at, (qw_ref[:, at] * keep - rate_q * ortho) * factor))
        for i, (ortho, factor) in enumerate(((even[24:32], r_even), (odd[24:32], r_odd))):
            at = pl.ds(pl.multiple_of(p * 256 + i * 128, 128), 128)
            done.append((kf_ref, at, (kw_ref[:, at] * keep - rate_k * ortho) * factor))
        return done

    def finish_group(k):
        done = []
        for i in range(pairs):
            done += finish(k * pairs + i)
        for ref, at, value in done:
            ref[:, at] = value

    span(back, home, 1, group - 1, back_sem, home_sem.at[0]).wait_recv()
    finish_group(0)

    @pl.loop(1, groups)
    def _(k):
        span(back, home, k * group, group, back_sem, home_sem.at[k]).wait_recv()
        finish_group(k)

    span(send, recv, 1, owners - 1, send_sem, recv_sem.at[0]).wait_send()
    span(back, home, 1, owners - 1, back_sem, home_sem.at[0]).wait_send()


def emit(*refs):
    sem = refs[8]
    copies = [pltpu.make_async_copy(refs[i], refs[4 + i], sem.at[i]) for i in range(4)]
    for copy in copies:
        copy.start()
    for copy in copies:
        copy.wait()


def local(
    logit_partial,
    head_order,
    query_weight,
    query_moment,
    query_grad,
    key_weight,
    key_moment,
    key_grad,
):
    owners = lax.axis_size("zero")
    n_ctx = lax.axis_size("ctx")
    group = 8 if owners == 64 else 2
    groups = owners // group
    heads = head_order.shape[1]
    query, key = query_weight.shape[1:], key_weight.shape[1:]
    vmem = pl.BlockSpec(memory_space=pltpu.VMEM)
    hbm = pl.BlockSpec(memory_space=pltpu.HBM)
    dma = pltpu.SemaphoreType.DMA
    shapes = (
        jax.ShapeDtypeStruct(query, jnp.float32),
        jax.ShapeDtypeStruct(query, jnp.bfloat16),
        jax.ShapeDtypeStruct(key, jnp.float32),
        jax.ShapeDtypeStruct(key, jnp.bfloat16),
    )
    results = pl.pallas_call(
        functools.partial(body, owners, n_ctx),
        out_shape=shapes,
        in_specs=[hbm] * 8,
        out_specs=(vmem, vmem, vmem, vmem),
        scratch_shapes=[
            pltpu.VMEM((owners, ROWS, LANES), jnp.bfloat16),
            pltpu.VMEM((owners, ROWS, LANES), jnp.bfloat16),
            pltpu.VMEM((owners, ROWS, LANES), jnp.bfloat16),
            pltpu.VMEM((owners, ROWS, LANES), jnp.bfloat16),
            pltpu.VMEM((owners * 32, 384), jnp.bfloat16),
            pltpu.VMEM((768, 256), jnp.bfloat16),
            pltpu.VMEM((256, 256), jnp.float32),
            pltpu.VMEM((128, 128), jnp.float32),
            pltpu.VMEM((n_ctx, 8, LANES), jnp.float32),
            pltpu.VMEM((n_ctx, 8, LANES), jnp.float32),
            pltpu.VMEM((heads, LANES), jnp.float32),
            pltpu.VMEM((heads, LANES), jnp.float32),
            pltpu.VMEM(query, jnp.float32),
            pltpu.VMEM(key, jnp.float32),
            pltpu.VMEM(query, jnp.bfloat16),
            pltpu.VMEM(query, jnp.bfloat16),
            pltpu.VMEM(key, jnp.bfloat16),
            pltpu.VMEM(key, jnp.bfloat16),
            pltpu.VMEM(logit_partial.shape[1:], jnp.float32),
            pltpu.VMEM(head_order.shape, jnp.int32),
            dma,
            dma((groups,)),
            dma,
            dma((groups,)),
            dma,
            dma,
            dma((8,)),
        ],
        compiler_params=pltpu.CompilerParams(
            collective_id=0, has_side_effects=True, vmem_limit_bytes=48 * 1024 * 1024
        ),
        name="muon",
    )(
        *(
            pltpu.with_memory_space_constraint(array, pltpu.HBM)
            for array in (
                logit_partial[0],
                head_order,
                query_weight[0],
                query_moment[0],
                query_grad[0],
                key_weight[0],
                key_moment[0],
                key_grad[0],
            )
        )
    )
    results = pl.pallas_call(
        emit,
        out_shape=shapes,
        in_specs=[vmem] * 4,
        out_specs=[hbm] * 4,
        scratch_shapes=[dma((4,))],
        compiler_params=pltpu.CompilerParams(vmem_limit_bytes=8 * 1024 * 1024),
        name="emit",
    )(*(pltpu.with_memory_space_constraint(result, pltpu.VMEM) for result in results))
    return tuple(result[None] for result in results)


def solution(mesh):
    shard = P("ctx", "zero", None)
    return jax.shard_map(
        local,
        mesh=mesh,
        in_specs=(P("ctx", None, None), P(), shard, shard, shard, shard, shard, shard),
        out_specs=(shard, shard, shard, shard),
        check_vma=False,
    )
```

```python
import functools
import math

import jax
import jax.numpy as jnp
from jax import lax
from jax.experimental import pallas as pl
from jax.experimental.pallas import tpu as pltpu
from jax.sharding import PartitionSpec as P

QR = 1536
KR = 512
NOPE = 128
ROPE = 64
WIDTH = NOPE + ROPE
ITERS = 5
LANES = 128
ROWS = 48


MOMENTUM_DECAY = 0.95
LEARN_RATE = 0.02
WEIGHT_DECAY = 0.1
CLIP_LIMIT = 100.0
NEWTON_FIRST = 3.4445
NEWTON_SECOND = -4.775
NEWTON_THIRD = 2.0315
NORM_EPSILON = 1e-07
HIGHEST = lax.Precision.HIGHEST
MESH = pl.DeviceIdType.MESH


def gram_of(x):
    return lax.dot_general(x, x, (((0,), (0,)), ((), ())), preferred_element_type=jnp.float32)


def begin(gram, size):
    gram = gram[0:size]
    eye = lax.broadcasted_iota(jnp.int32, gram.shape, 0) == lax.broadcasted_iota(
        jnp.int32, gram.shape, 1
    )
    total = jnp.sum(jnp.where(eye, gram, 0.0), axis=1, keepdims=True)
    total = jnp.sum(total, axis=0, keepdims=True)
    inverse = 1.0 / (jnp.sqrt(total) + NORM_EPSILON)
    return gram * inverse * inverse, inverse, jnp.where(eye, 1.0, 0.0)


def square(x):
    missing = x.shape[1] - x.shape[0]
    if not missing:
        return x
    return jnp.concatenate([x, jnp.zeros((missing, x.shape[1]), x.dtype)], axis=0)


def split(m):
    high = m.astype(jnp.bfloat16)
    return high, (m - high.astype(jnp.float32)).astype(jnp.bfloat16)


def split3(m):
    high = m.astype(jnp.bfloat16)
    rest = m - high.astype(jnp.float32)
    middle = rest.astype(jnp.bfloat16)
    return high, middle, (rest - middle.astype(jnp.float32)).astype(jnp.bfloat16)


def joined(lefts, rights):
    return jnp.dot(
        jnp.concatenate(lefts, axis=1),
        jnp.concatenate([square(right) for right in rights], axis=0),
        preferred_element_type=jnp.float32,
    )


def mul3(a, b):
    return joined((a[0], a[0], a[1]), (b[0], b[1], b[0]))


def mul6(a, b):
    return joined((a[0], a[0], a[1], a[1], a[0], a[2]), (b[0], b[1], b[0], b[1], b[2], b[0]))


def stack(a, b):
    return tuple(jnp.concatenate(pair, axis=0) for pair in zip(a, b))


def newton(grams):
    a, inverse, eye = (list(x) for x in zip(*grams))
    m = [None] * len(a)
    which = range(len(a))
    for sweep in range(ITERS):
        exact = sweep == 0
        parts, product = (split3, mul6) if exact else (split, mul3)
        a_parts = [parts(a[i]) for i in which]
        s = [product(a_parts[i], a_parts[i]) for i in which]
        p = [NEWTON_FIRST * eye[i] + NEWTON_SECOND * a[i] + NEWTON_THIRD * s[i] for i in which]
        p_parts = [parts(p[i]) for i in which]
        if exact:
            y = [product(a_parts[i], p_parts[i]) for i in which]
            a = [product(parts(y[i]), p_parts[i]) for i in which]
            m = p
        elif sweep < ITERS - 1:
            both = [product(stack(a_parts[i], parts(m[i])), p_parts[i]) for i in which]
            size = [a[i].shape[0] for i in which]
            a = [product(parts(both[i][0 : size[i]]), p_parts[i]) for i in which]
            m = [both[i][size[i] :] for i in which]
        else:
            m = [product(parts(m[i]), p_parts[i]) for i in which]
    return [m[i] * inverse[i] for i in which]


def half_roll(x):
    return pltpu.roll(x, ROPE, 1)


def body(
    owners,
    n_ctx,
    lp_hbm,
    order_hbm,
    qw_hbm,
    qm_hbm,
    qg_hbm,
    kw_hbm,
    km_hbm,
    kg_hbm,
    qf_ref,
    qv_ref,
    kf_ref,
    kv_ref,
    send,
    recv,
    back,
    home,
    wide,
    factor,
    gram_q,
    gram_k,
    lsend,
    lrecv,
    gamma,
    root,
    qw_ref,
    kw_ref,
    qm_ref,
    qg_ref,
    km_ref,
    kg_ref,
    lp_ref,
    order_ref,
    send_sem,
    recv_sem,
    back_sem,
    home_sem,
    lsend_sem,
    lrecv_sem,
    load_sem,
):
    nx = 4 if owners == 64 else 1
    chips = owners // 2
    nz = chips // nx
    group = 2 * nx
    groups = owners // group
    pairs = group // 2
    me_c = lax.axis_index("ctx")
    me = lax.axis_index("zero")
    core = lax.rem(me, 2)
    chip = lax.div(me, 2)
    x0, z0 = lax.div(chip, nz), lax.rem(chip, nz)

    def core_at(dc):
        return lax.rem(core + dc, 2)

    def offset(t):
        far = lax.rem(chips - t, chips)
        i = lax.div(far, nx)
        dz = lax.div(i + 1, 2) * (1 - 2 * lax.rem(i + 1, 2))
        dx = lax.rem(far, nx)
        return dx, dz

    def chip_to(t):
        dx, dz = offset(t)
        way = 1 - 2 * core
        return lax.rem(x0 + way * dx + nx, nx) * nz + lax.rem(z0 + way * dz + nz, nz)

    def chip_from(t, dc):
        dx, dz = offset(t)
        way = 1 - 2 * core_at(dc)
        return lax.rem(x0 - way * dx + nx, nx) * nz + lax.rem(z0 - way * dz + nz, nz)

    loads = [
        pltpu.make_async_copy(source, target, load_sem.at[i])
        for i, (source, target) in enumerate(
            (
                (qm_hbm, qm_ref),
                (qg_hbm, qg_ref),
                (km_hbm, km_ref),
                (kg_hbm, kg_ref),
                (lp_hbm, lp_ref),
                (order_hbm, order_ref),
                (qw_hbm, qw_ref),
                (kw_hbm, kw_ref),
            )
        )
    ]
    for load in loads[:6]:
        load.start()

    barrier = pltpu.get_barrier_semaphore()

    @pl.loop(1, owners)
    def _(i):
        pl.semaphore_signal(
            barrier, inc=1, device_id=(me_c, lax.rem(me + i, owners)), device_id_type=MESH
        )

    @pl.loop(1, n_ctx)
    def _(i):
        pl.semaphore_signal(
            barrier, inc=1, device_id=(lax.rem(me_c + i, n_ctx), me), device_id_type=MESH
        )

    heads = lp_ref.shape[1]
    for load in loads[:4]:
        load.wait()
    for load in loads[6:]:
        load.start()
    lane16 = lax.broadcasted_iota(jnp.int32, (16, LANES), 1) < ROPE
    zero8 = jnp.zeros((8, LANES), jnp.float32)

    def make(t):
        p = chip_to(t)
        qs = pl.ds(pl.multiple_of(p * 384, 128), 384)
        ks = pl.ds(pl.multiple_of(p * 256, 128), 256)
        qv = (
            MOMENTUM_DECAY * qm_ref[:, qs].astype(jnp.float32) + qg_ref[:, qs].astype(jnp.float32)
        ).astype(jnp.bfloat16)
        kv = (
            MOMENTUM_DECAY * km_ref[:, ks].astype(jnp.float32) + kg_ref[:, ks].astype(jnp.float32)
        ).astype(jnp.bfloat16)
        qv_ref[:, qs] = qv
        kv_ref[:, ks] = kv
        qv = qv.astype(jnp.float32)
        kv = kv.astype(jnp.float32)
        middle = qv[:, 128:256]
        turned = half_roll(middle)
        low = jnp.concatenate([middle[16:24], zero8], axis=0)
        low_turned = jnp.concatenate([turned[16:24], zero8], axis=0)
        even = 2 * t + core
        odd = 2 * t + 1 - core
        send[even, 0:32, :] = jnp.concatenate([qv[:, 0:128], kv[:, 0:128]], axis=0).astype(
            jnp.bfloat16
        )
        send[even, 32:48, :] = jnp.where(lane16, middle[0:16], low_turned).astype(jnp.bfloat16)
        send[odd, 0:32, :] = jnp.concatenate([qv[:, 256:384], kv[:, 128:256]], axis=0).astype(
            jnp.bfloat16
        )
        send[odd, 32:48, :] = jnp.where(lane16, turned[0:16], low).astype(jnp.bfloat16)

    def out_copy(t, dc):
        j = 2 * t + dc
        return pltpu.make_async_remote_copy(
            src_ref=send.at[j],
            dst_ref=recv.at[j],
            send_sem=send_sem,
            recv_sem=recv_sem.at[lax.div(j, group)],
            device_id=(me_c, 2 * chip_to(t) + core_at(dc)),
            device_id_type=MESH,
        )

    def back_copy(t, dc):
        j = 2 * t + dc
        return pltpu.make_async_remote_copy(
            src_ref=back.at[j],
            dst_ref=home.at[j],
            send_sem=back_sem,
            recv_sem=home_sem.at[lax.div(j, group)],
            device_id=(me_c, 2 * chip_from(t, dc) + core_at(dc)),
            device_id_type=MESH,
        )

    def span(buffer_out, buffer_in, first, size, out_sem, in_sem):
        return pltpu.make_async_remote_copy(
            src_ref=buffer_out.at[pl.ds(first, size)],
            dst_ref=buffer_in.at[pl.ds(first, size)],
            send_sem=out_sem,
            recv_sem=in_sem,
            device_id=(me_c, me),
            device_id_type=MESH,
        )

    make(0)
    recv[0] = send[0]
    pl.semaphore_wait(barrier, owners - 1 + n_ctx - 1)
    out_copy(0, 1).start()

    @pl.loop(1, chips)
    def _(t):
        make(t)
        out_copy(t, 0).start()
        out_copy(t, 1).start()

    loads[4].wait()
    for layer in range(n_ctx):
        lsend[layer, :, 0:heads] = jnp.broadcast_to(lp_ref[layer : layer + 1, :], (8, heads))
        lsend[layer, :, heads:] = jnp.zeros((8, LANES - heads), jnp.float32)

    @pl.loop(1, n_ctx)
    def _(i):
        other = lax.rem(me_c + i, n_ctx)
        pltpu.make_async_remote_copy(
            src_ref=lsend.at[other],
            dst_ref=lrecv.at[i],
            send_sem=lsend_sem,
            recv_sem=lrecv_sem,
            device_id=(other, me),
            device_id_type=MESH,
        ).start()

    rows = group * 32
    row = lax.rem(lax.broadcasted_iota(jnp.int32, (rows, LANES), 0), 32)
    is_query = row < 24
    lane = lax.broadcasted_iota(jnp.int32, (group * 16, LANES), 1) < ROPE

    def gather(k):
        first = pl.multiple_of(k * rows, rows)
        block = recv[pl.ds(k * group, group), 0:32, :].reshape(rows, LANES).astype(jnp.float32)
        third = recv[pl.ds(k * group, group), 32:48, :].reshape(group * 16, LANES)
        third = third.astype(jnp.float32)
        top = jnp.where(lane, third, 0.0).reshape(group, 16, LANES)
        bottom = jnp.where(lane, half_roll(third), 0.0).reshape(group, 16, LANES)
        third = jnp.concatenate([top, bottom], axis=1).reshape(rows, LANES)
        query = jnp.where(is_query, block, 0.0).astype(jnp.bfloat16)
        key = jnp.where(is_query, 0.0, block).astype(jnp.bfloat16)
        full = jnp.concatenate([query, third.astype(jnp.bfloat16)], axis=1)
        wide[pl.ds(first, rows), 0:256] = full
        wide[pl.ds(first, rows), 256:384] = key
        gram_q[...] += gram_of(full)
        gram_k[...] += gram_of(key)

    gram_q[...] = jnp.zeros_like(gram_q)
    gram_k[...] = jnp.zeros_like(gram_k)
    span(send, recv, 1, group - 1, send_sem, recv_sem.at[0]).wait_recv()
    gather(0)

    @pl.loop(1, groups)
    def _(k):
        span(send, recv, k * group, group, send_sem, recv_sem.at[k]).wait_recv()
        gather(k)

    mq, mk = newton([begin(gram_q[...], WIDTH), begin(gram_k[...], NOPE)])
    mq, mk = split(square(mq)), split(mk)
    for half in range(2):
        first = half * 384
        factor[first : first + 256, :] = mq[half]
        factor[first + 256 : first + 384, 0:128] = mk[half]
        factor[first + 256 : first + 384, 128:256] = jnp.zeros((128, 128), jnp.bfloat16)

    def give(k):
        first = pl.multiple_of(k * rows, rows)
        x = wide[pl.ds(first, rows), :]
        product = jnp.dot(
            jnp.concatenate([x, x], axis=1), factor[...], preferred_element_type=jnp.float32
        )
        block = product[:, 0:128]
        third = product[:, 128:256].reshape(group, 32, LANES)
        top = third[:, 0:16].reshape(group * 16, LANES)
        bottom = half_roll(third[:, 16:32].reshape(group * 16, LANES))
        third = jnp.where(lane, top, bottom)
        back[pl.ds(k * group, group), 0:32, :] = block.astype(jnp.bfloat16).reshape(
            group, 32, LANES
        )
        back[pl.ds(k * group, group), 32:48, :] = third.astype(jnp.bfloat16).reshape(
            group, 16, LANES
        )

    give(0)
    back_copy(0, 1).start()
    for t in range(1, pairs):
        back_copy(t, 0).start()
        back_copy(t, 1).start()
    home[0] = back[0]

    @pl.loop(1, groups)
    def _(k):
        give(k)

        @pl.loop(0, pairs)
        def _(i):
            back_copy(k * pairs + i, 0).start()
            back_copy(k * pairs + i, 1).start()

    lrecv[0] = lsend[me_c]
    pltpu.make_async_remote_copy(
        src_ref=lsend.at[pl.ds(1, n_ctx - 1)],
        dst_ref=lrecv.at[pl.ds(1, n_ctx - 1)],
        send_sem=lsend_sem,
        recv_sem=lrecv_sem,
        device_id=(me_c, me),
        device_id_type=MESH,
    ).wait()
    rowmax = jnp.max(lrecv[...], axis=0)[0:1, 0:heads]
    loads[5].wait()
    order = order_ref[pl.ds(me_c, 1), :]
    hit = jnp.broadcast_to(order, (heads, heads)) == lax.broadcasted_iota(
        jnp.int32, (heads, heads), 0
    )
    logit_max = jnp.sum(
        jnp.where(hit, jnp.broadcast_to(rowmax, (heads, heads)), 0.0), axis=1, keepdims=True
    )
    clip = jnp.minimum(1.0, CLIP_LIMIT / logit_max)
    gamma[...] = jnp.broadcast_to(clip, (heads, LANES))
    root[...] = jnp.broadcast_to(jnp.sqrt(clip), (heads, LANES))

    for load in loads[6:]:
        load.wait()
    keep = 1.0 - LEARN_RATE * WEIGHT_DECAY
    rate_q = LEARN_RATE * (0.2 * math.sqrt(max(QR, WIDTH)))
    rate_k = LEARN_RATE * (0.2 * math.sqrt(max(KR, NOPE)))
    lane1 = lax.broadcasted_iota(jnp.int32, (1, LANES), 1) < ROPE

    def finish(t):
        p = chip_to(t)
        even = home[2 * t + core].astype(jnp.float32)
        odd = home[2 * t + 1 - core].astype(jnp.float32)
        even_third, odd_third = even[32:48], odd[32:48]
        even_turned, odd_turned = half_roll(even_third), half_roll(odd_third)
        middle = jnp.concatenate(
            [
                jnp.where(lane16, even_third, odd_turned),
                jnp.where(lane16, even_turned, odd_third)[0:8],
            ],
            axis=0,
        )
        g_even, g_odd = gamma[pl.ds(2 * p, 1), :], gamma[pl.ds(2 * p + 1, 1), :]
        r_even, r_odd = root[pl.ds(2 * p, 1), :], root[pl.ds(2 * p + 1, 1), :]
        tiles = (
            (even[0:24], r_even),
            (middle, jnp.where(lane1, g_even, r_odd)),
            (odd[0:24], jnp.where(lane1, r_odd, g_odd)),
        )
        done = []
        for i, (ortho, factor) in enumerate(tiles):
            at = pl.ds(pl.multiple_of(p * 384 + i * 128, 128), 128)
            done.append((qf_ref, at, (qw_ref[:, at] * keep - rate_q * ortho) * factor))
        for i, (ortho, factor) in enumerate(((even[24:32], r_even), (odd[24:32], r_odd))):
            at = pl.ds(pl.multiple_of(p * 256 + i * 128, 128), 128)
            done.append((kf_ref, at, (kw_ref[:, at] * keep - rate_k * ortho) * factor))
        return done

    def finish_group(k):
        done = []
        for i in range(pairs):
            done += finish(k * pairs + i)
        for ref, at, value in done:
            ref[:, at] = value

    span(back, home, 1, group - 1, back_sem, home_sem.at[0]).wait_recv()
    finish_group(0)

    @pl.loop(1, groups)
    def _(k):
        span(back, home, k * group, group, back_sem, home_sem.at[k]).wait_recv()
        finish_group(k)

    span(send, recv, 1, owners - 1, send_sem, recv_sem.at[0]).wait_send()
    span(back, home, 1, owners - 1, back_sem, home_sem.at[0]).wait_send()


def emit(*refs):
    sem = refs[8]
    copies = [pltpu.make_async_copy(refs[i], refs[4 + i], sem.at[i]) for i in range(4)]
    for copy in copies:
        copy.start()
    for copy in copies:
        copy.wait()


def local(
    logit_partial,
    head_order,
    query_weight,
    query_moment,
    query_grad,
    key_weight,
    key_moment,
    key_grad,
):
    owners = lax.axis_size("zero")
    n_ctx = lax.axis_size("ctx")
    group = 8 if owners == 64 else 2
    groups = owners // group
    heads = head_order.shape[1]
    query, key = query_weight.shape[1:], key_weight.shape[1:]
    vmem = pl.BlockSpec(memory_space=pltpu.VMEM)
    hbm = pl.BlockSpec(memory_space=pltpu.HBM)
    dma = pltpu.SemaphoreType.DMA
    shapes = (
        jax.ShapeDtypeStruct(query, jnp.float32),
        jax.ShapeDtypeStruct(query, jnp.bfloat16),
        jax.ShapeDtypeStruct(key, jnp.float32),
        jax.ShapeDtypeStruct(key, jnp.bfloat16),
    )
    results = pl.pallas_call(
        functools.partial(body, owners, n_ctx),
        out_shape=shapes,
        in_specs=[hbm] * 8,
        out_specs=(vmem, vmem, vmem, vmem),
        scratch_shapes=[
            pltpu.VMEM((owners, ROWS, LANES), jnp.bfloat16),
            pltpu.VMEM((owners, ROWS, LANES), jnp.bfloat16),
            pltpu.VMEM((owners, ROWS, LANES), jnp.bfloat16),
            pltpu.VMEM((owners, ROWS, LANES), jnp.bfloat16),
            pltpu.VMEM((owners * 32, 384), jnp.bfloat16),
            pltpu.VMEM((768, 256), jnp.bfloat16),
            pltpu.VMEM((256, 256), jnp.float32),
            pltpu.VMEM((128, 128), jnp.float32),
            pltpu.VMEM((n_ctx, 8, LANES), jnp.float32),
            pltpu.VMEM((n_ctx, 8, LANES), jnp.float32),
            pltpu.VMEM((heads, LANES), jnp.float32),
            pltpu.VMEM((heads, LANES), jnp.float32),
            pltpu.VMEM(query, jnp.float32),
            pltpu.VMEM(key, jnp.float32),
            pltpu.VMEM(query, jnp.bfloat16),
            pltpu.VMEM(query, jnp.bfloat16),
            pltpu.VMEM(key, jnp.bfloat16),
            pltpu.VMEM(key, jnp.bfloat16),
            pltpu.VMEM(logit_partial.shape[1:], jnp.float32),
            pltpu.VMEM(head_order.shape, jnp.int32),
            dma,
            dma((groups,)),
            dma,
            dma((groups,)),
            dma,
            dma,
            dma((8,)),
        ],
        compiler_params=pltpu.CompilerParams(
            collective_id=0, has_side_effects=True, vmem_limit_bytes=48 * 1024 * 1024
        ),
        name="muon",
    )(
        *(
            pltpu.with_memory_space_constraint(array, pltpu.HBM)
            for array in (
                logit_partial[0],
                head_order,
                query_weight[0],
                query_moment[0],
                query_grad[0],
                key_weight[0],
                key_moment[0],
                key_grad[0],
            )
        )
    )
    results = pl.pallas_call(
        emit,
        out_shape=shapes,
        in_specs=[vmem] * 4,
        out_specs=[hbm] * 4,
        scratch_shapes=[dma((4,))],
        compiler_params=pltpu.CompilerParams(vmem_limit_bytes=8 * 1024 * 1024),
        name="emit",
    )(*(pltpu.with_memory_space_constraint(result, pltpu.VMEM) for result in results))
    return tuple(result[None] for result in results)


def solution(mesh):
    shard = P("ctx", "zero", None)
    return jax.shard_map(
        local,
        mesh=mesh,
        in_specs=(P("ctx", None, None), P(), shard, shard, shard, shard, shard, shard),
        out_specs=(shard, shard, shard, shard),
        check_vma=False,
    )
```

```python
import functools
import math

import jax
import jax.numpy as jnp
from jax import lax
from jax.experimental import pallas as pl
from jax.experimental.pallas import tpu as pltpu
from jax.sharding import PartitionSpec as P

QR = 1536
KR = 512
NOPE = 128
ROPE = 64
WIDTH = NOPE + ROPE
ITERS = 5
LANES = 128
ROWS = 48


MOMENTUM_DECAY = 0.95
LEARN_RATE = 0.02
WEIGHT_DECAY = 0.1
CLIP_LIMIT = 100.0
NEWTON_FIRST = 3.4445
NEWTON_SECOND = -4.775
NEWTON_THIRD = 2.0315
NORM_EPSILON = 1e-07
HIGHEST = lax.Precision.HIGHEST
MESH = pl.DeviceIdType.MESH


def gram_of(x):
    return lax.dot_general(x, x, (((0,), (0,)), ((), ())), preferred_element_type=jnp.float32)


def begin(gram, size):
    gram = gram[0:size]
    eye = lax.broadcasted_iota(jnp.int32, gram.shape, 0) == lax.broadcasted_iota(
        jnp.int32, gram.shape, 1
    )
    total = jnp.sum(jnp.where(eye, gram, 0.0), axis=1, keepdims=True)
    total = jnp.sum(total, axis=0, keepdims=True)
    inverse = 1.0 / (jnp.sqrt(total) + NORM_EPSILON)
    return gram * inverse * inverse, inverse, jnp.where(eye, 1.0, 0.0)


def square(x):
    missing = x.shape[1] - x.shape[0]
    if not missing:
        return x
    return jnp.concatenate([x, jnp.zeros((missing, x.shape[1]), x.dtype)], axis=0)


def split(m):
    high = m.astype(jnp.bfloat16)
    return high, (m - high.astype(jnp.float32)).astype(jnp.bfloat16)


def split3(m):
    high = m.astype(jnp.bfloat16)
    rest = m - high.astype(jnp.float32)
    middle = rest.astype(jnp.bfloat16)
    return high, middle, (rest - middle.astype(jnp.float32)).astype(jnp.bfloat16)


def joined(lefts, rights):
    return jnp.dot(
        jnp.concatenate(lefts, axis=1),
        jnp.concatenate([square(right) for right in rights], axis=0),
        preferred_element_type=jnp.float32,
    )


def mul3(a, b):
    return joined((a[0], a[0], a[1]), (b[0], b[1], b[0]))


def mul6(a, b):
    return joined((a[0], a[0], a[1], a[1], a[0], a[2]), (b[0], b[1], b[0], b[1], b[2], b[0]))


def newton(grams):
    a, inverse, eye = (list(x) for x in zip(*grams))
    m = [None] * len(a)
    which = range(len(a))
    for sweep in range(ITERS):
        exact = sweep == 0
        parts, product = (split3, mul6) if exact else (split, mul3)
        a_parts = [parts(a[i]) for i in which]
        s = [product(a_parts[i], a_parts[i]) for i in which]
        p = [NEWTON_FIRST * eye[i] + NEWTON_SECOND * a[i] + NEWTON_THIRD * s[i] for i in which]
        p_parts = [parts(p[i]) for i in which]
        if exact:
            y = [product(a_parts[i], p_parts[i]) for i in which]
            a = [product(parts(y[i]), p_parts[i]) for i in which]
            m = p
        elif sweep < ITERS - 1:
            y = [product(a_parts[i], p_parts[i]) for i in which]
            m = [product(parts(m[i]), p_parts[i]) for i in which]
            a = [product(parts(y[i]), p_parts[i]) for i in which]
        else:
            m = [product(parts(m[i]), p_parts[i]) for i in which]
    return [m[i] * inverse[i] for i in which]


def half_roll(x):
    return pltpu.roll(x, ROPE, 1)


def body(
    owners,
    n_ctx,
    lp_hbm,
    order_hbm,
    qw_hbm,
    qm_hbm,
    qg_hbm,
    kw_hbm,
    km_hbm,
    kg_hbm,
    qf_ref,
    qv_ref,
    kf_ref,
    kv_ref,
    send,
    recv,
    back,
    home,
    wide,
    factor,
    gram_q,
    gram_k,
    lsend,
    lrecv,
    gamma,
    root,
    qw_ref,
    kw_ref,
    qm_ref,
    qg_ref,
    km_ref,
    kg_ref,
    lp_ref,
    order_ref,
    send_sem,
    recv_sem,
    back_sem,
    home_sem,
    lsend_sem,
    lrecv_sem,
    load_sem,
):
    nx = 4 if owners == 64 else 1
    chips = owners // 2
    nz = chips // nx
    group = 2 * nx
    groups = owners // group
    pairs = group // 2
    me_c = lax.axis_index("ctx")
    me = lax.axis_index("zero")
    core = lax.rem(me, 2)
    chip = lax.div(me, 2)
    x0, z0 = lax.div(chip, nz), lax.rem(chip, nz)

    def core_at(dc):
        return lax.rem(core + dc, 2)

    def offset(t):
        far = lax.rem(chips - t, chips)
        i = lax.div(far, nx)
        dz = lax.div(i + 1, 2) * (1 - 2 * lax.rem(i + 1, 2))
        dx = lax.rem(far, nx)
        return dx, dz

    def chip_to(t):
        dx, dz = offset(t)
        way = 1 - 2 * core
        return lax.rem(x0 + way * dx + nx, nx) * nz + lax.rem(z0 + way * dz + nz, nz)

    def chip_from(t, dc):
        dx, dz = offset(t)
        way = 1 - 2 * core_at(dc)
        return lax.rem(x0 - way * dx + nx, nx) * nz + lax.rem(z0 - way * dz + nz, nz)

    loads = [
        pltpu.make_async_copy(source, target, load_sem.at[i])
        for i, (source, target) in enumerate(
            (
                (qm_hbm, qm_ref),
                (qg_hbm, qg_ref),
                (km_hbm, km_ref),
                (kg_hbm, kg_ref),
                (lp_hbm, lp_ref),
                (order_hbm, order_ref),
                (qw_hbm, qw_ref),
                (kw_hbm, kw_ref),
            )
        )
    ]
    for load in loads[:6]:
        load.start()

    barrier = pltpu.get_barrier_semaphore()

    @pl.loop(1, owners)
    def _(i):
        pl.semaphore_signal(
            barrier, inc=1, device_id=(me_c, lax.rem(me + i, owners)), device_id_type=MESH
        )

    @pl.loop(1, n_ctx)
    def _(i):
        pl.semaphore_signal(
            barrier, inc=1, device_id=(lax.rem(me_c + i, n_ctx), me), device_id_type=MESH
        )

    heads = lp_ref.shape[1]
    for load in loads[:4]:
        load.wait()
    for load in loads[6:]:
        load.start()
    lane16 = lax.broadcasted_iota(jnp.int32, (16, LANES), 1) < ROPE
    zero8 = jnp.zeros((8, LANES), jnp.float32)

    def make(t):
        p = chip_to(t)
        qs = pl.ds(pl.multiple_of(p * 384, 128), 384)
        ks = pl.ds(pl.multiple_of(p * 256, 128), 256)
        qv = (
            MOMENTUM_DECAY * qm_ref[:, qs].astype(jnp.float32) + qg_ref[:, qs].astype(jnp.float32)
        ).astype(jnp.bfloat16)
        kv = (
            MOMENTUM_DECAY * km_ref[:, ks].astype(jnp.float32) + kg_ref[:, ks].astype(jnp.float32)
        ).astype(jnp.bfloat16)
        qv_ref[:, qs] = qv
        kv_ref[:, ks] = kv
        qv = qv.astype(jnp.float32)
        kv = kv.astype(jnp.float32)
        middle = qv[:, 128:256]
        turned = half_roll(middle)
        low = jnp.concatenate([middle[16:24], zero8], axis=0)
        low_turned = jnp.concatenate([turned[16:24], zero8], axis=0)
        even = 2 * t + core
        odd = 2 * t + 1 - core
        send[even, 0:32, :] = jnp.concatenate([qv[:, 0:128], kv[:, 0:128]], axis=0).astype(
            jnp.bfloat16
        )
        send[even, 32:48, :] = jnp.where(lane16, middle[0:16], low_turned).astype(jnp.bfloat16)
        send[odd, 0:32, :] = jnp.concatenate([qv[:, 256:384], kv[:, 128:256]], axis=0).astype(
            jnp.bfloat16
        )
        send[odd, 32:48, :] = jnp.where(lane16, turned[0:16], low).astype(jnp.bfloat16)

    def out_copy(t, dc):
        j = 2 * t + dc
        return pltpu.make_async_remote_copy(
            src_ref=send.at[j],
            dst_ref=recv.at[j],
            send_sem=send_sem,
            recv_sem=recv_sem.at[lax.div(j, group)],
            device_id=(me_c, 2 * chip_to(t) + core_at(dc)),
            device_id_type=MESH,
        )

    def back_copy(t, dc):
        j = 2 * t + dc
        return pltpu.make_async_remote_copy(
            src_ref=back.at[j],
            dst_ref=home.at[j],
            send_sem=back_sem,
            recv_sem=home_sem.at[lax.div(j, group)],
            device_id=(me_c, 2 * chip_from(t, dc) + core_at(dc)),
            device_id_type=MESH,
        )

    def span(buffer_out, buffer_in, first, size, out_sem, in_sem):
        return pltpu.make_async_remote_copy(
            src_ref=buffer_out.at[pl.ds(first, size)],
            dst_ref=buffer_in.at[pl.ds(first, size)],
            send_sem=out_sem,
            recv_sem=in_sem,
            device_id=(me_c, me),
            device_id_type=MESH,
        )

    make(0)
    recv[0] = send[0]
    pl.semaphore_wait(barrier, owners - 1 + n_ctx - 1)
    out_copy(0, 1).start()

    @pl.loop(1, chips)
    def _(t):
        make(t)
        out_copy(t, 0).start()
        out_copy(t, 1).start()

    loads[4].wait()
    for layer in range(n_ctx):
        lsend[layer, :, 0:heads] = jnp.broadcast_to(lp_ref[layer : layer + 1, :], (8, heads))
        lsend[layer, :, heads:] = jnp.zeros((8, LANES - heads), jnp.float32)

    @pl.loop(1, n_ctx)
    def _(i):
        other = lax.rem(me_c + i, n_ctx)
        pltpu.make_async_remote_copy(
            src_ref=lsend.at[other],
            dst_ref=lrecv.at[i],
            send_sem=lsend_sem,
            recv_sem=lrecv_sem,
            device_id=(other, me),
            device_id_type=MESH,
        ).start()

    rows = group * 32
    row = lax.rem(lax.broadcasted_iota(jnp.int32, (rows, LANES), 0), 32)
    is_query = row < 24
    lane = lax.broadcasted_iota(jnp.int32, (group * 16, LANES), 1) < ROPE

    def gather(k):
        first = pl.multiple_of(k * rows, rows)
        block = recv[pl.ds(k * group, group), 0:32, :].reshape(rows, LANES).astype(jnp.float32)
        third = recv[pl.ds(k * group, group), 32:48, :].reshape(group * 16, LANES)
        third = third.astype(jnp.float32)
        top = jnp.where(lane, third, 0.0).reshape(group, 16, LANES)
        bottom = jnp.where(lane, half_roll(third), 0.0).reshape(group, 16, LANES)
        third = jnp.concatenate([top, bottom], axis=1).reshape(rows, LANES)
        query = jnp.where(is_query, block, 0.0).astype(jnp.bfloat16)
        key = jnp.where(is_query, 0.0, block).astype(jnp.bfloat16)
        full = jnp.concatenate([query, third.astype(jnp.bfloat16)], axis=1)
        wide[pl.ds(first, rows), 0:256] = full
        wide[pl.ds(first, rows), 256:384] = key
        gram_q[...] += gram_of(full)
        gram_k[...] += gram_of(key)

    gram_q[...] = jnp.zeros_like(gram_q)
    gram_k[...] = jnp.zeros_like(gram_k)
    span(send, recv, 1, group - 1, send_sem, recv_sem.at[0]).wait_recv()
    gather(0)

    @pl.loop(1, groups)
    def _(k):
        span(send, recv, k * group, group, send_sem, recv_sem.at[k]).wait_recv()
        gather(k)

    mq, mk = newton([begin(gram_q[...], WIDTH), begin(gram_k[...], NOPE)])
    mq, mk = split(square(mq)), split(mk)
    for half in range(2):
        first = half * 384
        factor[first : first + 256, :] = mq[half]
        factor[first + 256 : first + 384, 0:128] = mk[half]
        factor[first + 256 : first + 384, 128:256] = jnp.zeros((128, 128), jnp.bfloat16)

    def give(k):
        first = pl.multiple_of(k * rows, rows)
        x = wide[pl.ds(first, rows), :]
        product = jnp.dot(
            jnp.concatenate([x, x], axis=1), factor[...], preferred_element_type=jnp.float32
        )
        block = product[:, 0:128]
        third = product[:, 128:256].reshape(group, 32, LANES)
        top = third[:, 0:16].reshape(group * 16, LANES)
        bottom = half_roll(third[:, 16:32].reshape(group * 16, LANES))
        third = jnp.where(lane, top, bottom)
        back[pl.ds(k * group, group), 0:32, :] = block.astype(jnp.bfloat16).reshape(
            group, 32, LANES
        )
        back[pl.ds(k * group, group), 32:48, :] = third.astype(jnp.bfloat16).reshape(
            group, 16, LANES
        )

    give(0)
    back_copy(0, 1).start()
    for t in range(1, pairs):
        back_copy(t, 0).start()
        back_copy(t, 1).start()
    home[0] = back[0]

    @pl.loop(1, groups)
    def _(k):
        give(k)

        @pl.loop(0, pairs)
        def _(i):
            back_copy(k * pairs + i, 0).start()
            back_copy(k * pairs + i, 1).start()

    lrecv[0] = lsend[me_c]
    pltpu.make_async_remote_copy(
        src_ref=lsend.at[pl.ds(1, n_ctx - 1)],
        dst_ref=lrecv.at[pl.ds(1, n_ctx - 1)],
        send_sem=lsend_sem,
        recv_sem=lrecv_sem,
        device_id=(me_c, me),
        device_id_type=MESH,
    ).wait()
    rowmax = jnp.max(lrecv[...], axis=0)[0:1, 0:heads]
    loads[5].wait()
    order = order_ref[pl.ds(me_c, 1), :]
    hit = jnp.broadcast_to(order, (heads, heads)) == lax.broadcasted_iota(
        jnp.int32, (heads, heads), 0
    )
    logit_max = jnp.sum(
        jnp.where(hit, jnp.broadcast_to(rowmax, (heads, heads)), 0.0), axis=1, keepdims=True
    )
    clip = jnp.minimum(1.0, CLIP_LIMIT / logit_max)
    gamma[...] = jnp.broadcast_to(clip, (heads, LANES))
    root[...] = jnp.broadcast_to(jnp.sqrt(clip), (heads, LANES))

    for load in loads[6:]:
        load.wait()
    keep = 1.0 - LEARN_RATE * WEIGHT_DECAY
    rate_q = LEARN_RATE * (0.2 * math.sqrt(max(QR, WIDTH)))
    rate_k = LEARN_RATE * (0.2 * math.sqrt(max(KR, NOPE)))
    lane1 = lax.broadcasted_iota(jnp.int32, (1, LANES), 1) < ROPE

    def finish(t):
        p = chip_to(t)
        even = home[2 * t + core].astype(jnp.float32)
        odd = home[2 * t + 1 - core].astype(jnp.float32)
        even_third, odd_third = even[32:48], odd[32:48]
        even_turned, odd_turned = half_roll(even_third), half_roll(odd_third)
        middle = jnp.concatenate(
            [
                jnp.where(lane16, even_third, odd_turned),
                jnp.where(lane16, even_turned, odd_third)[0:8],
            ],
            axis=0,
        )
        g_even, g_odd = gamma[pl.ds(2 * p, 1), :], gamma[pl.ds(2 * p + 1, 1), :]
        r_even, r_odd = root[pl.ds(2 * p, 1), :], root[pl.ds(2 * p + 1, 1), :]
        tiles = (
            (even[0:24], r_even),
            (middle, jnp.where(lane1, g_even, r_odd)),
            (odd[0:24], jnp.where(lane1, r_odd, g_odd)),
        )
        done = []
        for i, (ortho, factor) in enumerate(tiles):
            at = pl.ds(pl.multiple_of(p * 384 + i * 128, 128), 128)
            done.append((qf_ref, at, (qw_ref[:, at] * keep - rate_q * ortho) * factor))
        for i, (ortho, factor) in enumerate(((even[24:32], r_even), (odd[24:32], r_odd))):
            at = pl.ds(pl.multiple_of(p * 256 + i * 128, 128), 128)
            done.append((kf_ref, at, (kw_ref[:, at] * keep - rate_k * ortho) * factor))
        return done

    def finish_group(k):
        done = []
        for i in range(pairs):
            done += finish(k * pairs + i)
        for ref, at, value in done:
            ref[:, at] = value

    span(back, home, 1, group - 1, back_sem, home_sem.at[0]).wait_recv()
    finish_group(0)

    @pl.loop(1, groups)
    def _(k):
        span(back, home, k * group, group, back_sem, home_sem.at[k]).wait_recv()
        finish_group(k)

    span(send, recv, 1, owners - 1, send_sem, recv_sem.at[0]).wait_send()
    span(back, home, 1, owners - 1, back_sem, home_sem.at[0]).wait_send()


def emit(*refs):
    sem = refs[8]
    copies = [pltpu.make_async_copy(refs[i], refs[4 + i], sem.at[i]) for i in range(4)]
    for copy in copies:
        copy.start()
    for copy in copies:
        copy.wait()


def local(
    logit_partial,
    head_order,
    query_weight,
    query_moment,
    query_grad,
    key_weight,
    key_moment,
    key_grad,
):
    owners = lax.axis_size("zero")
    n_ctx = lax.axis_size("ctx")
    group = 8 if owners == 64 else 2
    groups = owners // group
    heads = head_order.shape[1]
    query, key = query_weight.shape[1:], key_weight.shape[1:]
    vmem = pl.BlockSpec(memory_space=pltpu.VMEM)
    hbm = pl.BlockSpec(memory_space=pltpu.HBM)
    dma = pltpu.SemaphoreType.DMA
    shapes = (
        jax.ShapeDtypeStruct(query, jnp.float32),
        jax.ShapeDtypeStruct(query, jnp.bfloat16),
        jax.ShapeDtypeStruct(key, jnp.float32),
        jax.ShapeDtypeStruct(key, jnp.bfloat16),
    )
    results = pl.pallas_call(
        functools.partial(body, owners, n_ctx),
        out_shape=shapes,
        in_specs=[hbm] * 8,
        out_specs=(vmem, vmem, vmem, vmem),
        scratch_shapes=[
            pltpu.VMEM((owners, ROWS, LANES), jnp.bfloat16),
            pltpu.VMEM((owners, ROWS, LANES), jnp.bfloat16),
            pltpu.VMEM((owners, ROWS, LANES), jnp.bfloat16),
            pltpu.VMEM((owners, ROWS, LANES), jnp.bfloat16),
            pltpu.VMEM((owners * 32, 384), jnp.bfloat16),
            pltpu.VMEM((768, 256), jnp.bfloat16),
            pltpu.VMEM((256, 256), jnp.float32),
            pltpu.VMEM((128, 128), jnp.float32),
            pltpu.VMEM((n_ctx, 8, LANES), jnp.float32),
            pltpu.VMEM((n_ctx, 8, LANES), jnp.float32),
            pltpu.VMEM((heads, LANES), jnp.float32),
            pltpu.VMEM((heads, LANES), jnp.float32),
            pltpu.VMEM(query, jnp.float32),
            pltpu.VMEM(key, jnp.float32),
            pltpu.VMEM(query, jnp.bfloat16),
            pltpu.VMEM(query, jnp.bfloat16),
            pltpu.VMEM(key, jnp.bfloat16),
            pltpu.VMEM(key, jnp.bfloat16),
            pltpu.VMEM(logit_partial.shape[1:], jnp.float32),
            pltpu.VMEM(head_order.shape, jnp.int32),
            dma,
            dma((groups,)),
            dma,
            dma((groups,)),
            dma,
            dma,
            dma((8,)),
        ],
        compiler_params=pltpu.CompilerParams(
            collective_id=0, has_side_effects=True, vmem_limit_bytes=48 * 1024 * 1024
        ),
        name="muon",
    )(
        *(
            pltpu.with_memory_space_constraint(array, pltpu.HBM)
            for array in (
                logit_partial[0],
                head_order,
                query_weight[0],
                query_moment[0],
                query_grad[0],
                key_weight[0],
                key_moment[0],
                key_grad[0],
            )
        )
    )
    results = pl.pallas_call(
        emit,
        out_shape=shapes,
        in_specs=[vmem] * 4,
        out_specs=[hbm] * 4,
        scratch_shapes=[dma((4,))],
        compiler_params=pltpu.CompilerParams(vmem_limit_bytes=8 * 1024 * 1024),
        name="emit",
    )(*(pltpu.with_memory_space_constraint(result, pltpu.VMEM) for result in results))
    return tuple(result[None] for result in results)


def solution(mesh):
    shard = P("ctx", "zero", None)
    return jax.shard_map(
        local,
        mesh=mesh,
        in_specs=(P("ctx", None, None), P(), shard, shard, shard, shard, shard, shard),
        out_specs=(shard, shard, shard, shard),
        check_vma=False,
    )
```
